32 devices in a mesh: rep: 16 (over z, x, core), exp: 2 (over y).
Axes of the slice: x: 2, y: 2, z: 4, core: 2. Of those that a mesh axis runs over, the one named last changes fastest.
Arguments:
- residual: bfloat16 [3, 64, 4096], P(None, ('rep', 'exp')), may hold values from -6 to 6
- queries: bfloat16 [3, 64, 4096], P(None, ('rep', 'exp')), may hold values from -30 to 30
- key_cache: bfloat16 [64, 1024, 256], P(('rep', 'exp')), may hold values from -6 to 6
- value_cache: bfloat16 [64, 1024, 256], P(('rep', 'exp')), may hold values from -6 to 6
- new_keys: bfloat16 [3, 64, 256], P(None, ('rep', 'exp')), may hold values from -6 to 6
- new_values: bfloat16 [3, 64, 256], P(None, ('rep', 'exp')), may hold values from -6 to 6
- cache_len: int32 [64], P(('rep', 'exp')), may hold values from 128 to 1024, as said below
- norm_gain: bfloat16 [4096], replicated, may hold values from 0.099609375 to 1.8984375
- expert_ids: int32 [3, 64, 8], P(None, ('rep', 'exp')), may hold values from 0 to 31, all different within a row; in each aligned block of 4 rows (0 to 3, 4 to 7, ..., all dimensions but the last counted through in order) at most 4 rows name the same one
- gate_scores: int32 [3, 64, 8], P(None, ('rep', 'exp')), may hold values from 1 to 1000
- gate_weight: bfloat16 [32, 1536, 4096], P('rep', 'exp'), may hold values from -0.09375 to 0.09375
- up_weight: bfloat16 [32, 1536, 4096], P('rep', 'exp'), may hold values from -0.09375 to 0.09375
- down_weight: bfloat16 [32, 1536, 4096], P('rep', 'exp'), may hold values from -0.15625 to 0.15625
Outputs:
- mixed: bfloat16 [3, 64, 4096], P(None, ('rep', 'exp'))
The draws below stay inside these ranges and needn't reach their ends.
Inputs may be any that keep to these rules, and one draw needn't show every extreme that they name: `expert_ids`: within each step and each aligned block of 4 sequences (the sequences of one index of rep), no expert is named more than 4 times, and that count is reached; a token names different experts. `cache_len`: some sequence holds all 1024 cached tokens.
All inputs are finite; a program needn't handle non-finite values.
Results may differ from the reference program's by a relative error of at most 0.013.
Values may be sent and summed in bfloat16 or wider, within the bound.
A program may use at most 128 MiB of HBM per device.

```python
import math
import jax
import jax.numpy as jnp
import numpy as np
from jax import lax

D = 4096
FF = 1536
HD = 128
QH = 32
KVH = 2
TOPK = 8
CAPE = 4
STEPS = 3
SEQ_DEV = 2
CACHE = 1024
BATCH = 64
EXPERTS = 32
N_REP = 16
N_EXP = 2


def draw_queries(key, part):
    drawn = jnp.clip(jax.random.normal(jax.random.fold_in(key, 31), (STEPS, BATCH, QH * HD), jnp.float32), -6.0, 6.0)
    return drawn.astype(jnp.bfloat16)


def draw_key_cache(key, part):
    drawn = jnp.clip(jax.random.normal(jax.random.fold_in(key, 11), (BATCH, CACHE, KVH * HD), jnp.float32), -6.0, 6.0)
    return drawn.astype(jnp.bfloat16)


def draw_cache_len(key, part):
    cache_lengths = jax.random.randint(jax.random.fold_in(key, 21), (BATCH,), CACHE // 8, CACHE + 1)
    longest = jax.random.randint(jax.random.fold_in(key, 22), (), 0, BATCH)
    return cache_lengths.at[longest].set(CACHE)


def set_ends(drawn, key, low, top_value):
    longest = drawn.shape.index(max(drawn.shape))
    spots = []
    for shift in (0, 1):
        where = [jax.random.randint(jax.random.fold_in(key, axis), (), 0, length) for axis, length in enumerate(drawn.shape)]
        where[longest] = (where[longest] + shift) % drawn.shape[longest]
        spots.append(tuple(where))
    return drawn.at[spots[0]].set(low).at[spots[1]].set(top_value)


def block_levels(own_key, shape, shards, least, top_value):
    level, own = 1.0, jax.random.fold_in(own_key, 6)
    for dim, parts in shards:
        draws = jnp.exp(jax.random.uniform(jax.random.fold_in(own, dim), (parts,), jnp.float32, least / len(shards), top_value / len(shards)))
        level = level * jnp.repeat(draws, shape[dim] // parts).reshape([-1 if axis == dim else 1 for axis in range(len(shape))])
    return level


def assign_block(stream_key, own, number, rows, amount, top, reach, skew):
    order = jax.random.permutation(stream_key, amount)
    crowded, usual = shares(amount, rows * top, reach, skew, True), shares(amount, rows * top, reach, skew, False)
    places = jnp.arange(amount)

    def named(lengths, rotation):
        used = int((lengths > 0).sum())
        fixed = max(1, used // 4)
        shifted = fixed + (places - fixed + rotation * (used - fixed)) % max(1, amount - fixed)
        return jnp.zeros((amount,), jnp.int32).at[order[jnp.where(places < fixed, places, shifted)]].set(jnp.asarray(lengths, jnp.int32))

    lengths = jnp.where(number % 4 == 0, named(crowded, number // 4), named(usual, number - number // 4 - 1))
    mixed = jax.random.permutation(jax.random.fold_in(own, 3), amount)
    giver, sink = mixed[0:amount // 2 * 2:2], mixed[1:amount // 2 * 2:2]
    slack = jnp.minimum(lengths[giver] - 1, reach - lengths[sink]) // 2
    slack = jnp.where((giver == order[0]) | (sink == order[0]) | (lengths[sink] == 0), 0, jnp.maximum(slack, 0))
    shifted = jax.random.randint(jax.random.fold_in(own, 4), (amount // 2,), 0, 1 << 20) % (slack + 1)
    lengths = lengths.at[giver].add(-shifted).at[sink].add(shifted)
    labels = jnp.searchsorted(jnp.cumsum(lengths), jnp.arange(rows * top), side="right").astype(jnp.int32)
    grid = labels.reshape(top, rows).T
    grid = grid[jax.random.permutation(jax.random.fold_in(own, 1), rows)]
    rotation = jax.random.randint(jax.random.fold_in(own, 2), (rows, 1), 0, top)
    return jnp.take_along_axis(grid, (jnp.arange(top)[None, :] + rotation) % top, axis=1)


def shares(count, total, bound, skew, full):
    loads = [(1 << 20) // math.isqrt(grade ** skew) + 1 for grade in range(1, count + 1)]
    largest = bound if full else min(bound, max(-(-total // count), total * loads[0] // sum(loads)))
    least = 1 if total - largest >= count - 1 else 0
    holding, rest = [largest] + [least] * (count - 1), total - largest - least * (count - 1)
    while rest > 0:
        candidates = [i for i in range(1, count) if holding[i] < largest] or [i for i in range(1, count) if holding[i] < bound]
        mass, budget = sum([loads[i] for i in candidates]), rest
        for i in candidates:
            extra = min(bound - holding[i], max(1, budget * loads[i] // mass), rest)
            holding[i] = holding[i] + extra
            rest = rest - extra
    return np.array(holding)


def scatter_about(rng, extent, deviation, reach, pieces=(), kind=jnp.bfloat16):
    drawn = deviation * jax.random.normal(rng, extent, jnp.float32)
    if pieces:
        drawn = drawn * block_levels(rng, extent, pieces, -0.22, 0.18)
    return jnp.clip(drawn, -reach, reach).astype(kind)


def setup_inputs(seed: int = 0) -> dict:
    arg_keys = jax.random.split(jax.random.key(seed), 14)
    residual = scatter_about(arg_keys[0], (STEPS, BATCH, D), 0.5, 6.0, ((1, 32),))
    queries = draw_queries(jax.random.fold_in(arg_keys[13], 71), 0)
    key_cache = draw_key_cache(jax.random.fold_in(arg_keys[13], 71), 0)
    value_cache = scatter_about(arg_keys[3], (BATCH, CACHE, KVH * HD), 1.0, 6.0, ((0, 32),))
    new_keys = scatter_about(arg_keys[4], (STEPS, BATCH, KVH * HD), 1.0, 6.0, ((1, 32),))
    new_values = scatter_about(arg_keys[5], (STEPS, BATCH, KVH * HD), 1.0, 6.0, ((1, 32),))
    cache_len = draw_cache_len(jax.random.fold_in(arg_keys[13], 71), 0)
    norm_gain = jnp.clip(1.0 + 0.18 * jax.random.normal(arg_keys[7], (D,), jnp.float32), 0.099609375, 1.8984375).astype(jnp.bfloat16)
    expert_ids_keys = jax.random.split(jax.random.fold_in(arg_keys[8], 1), STEPS * BATCH // (N_EXP * SEQ_DEV))
    expert_ids_turns = jax.random.permutation(jax.random.fold_in(arg_keys[8], 3), STEPS * BATCH // (N_EXP * SEQ_DEV))
    expert_ids = jax.vmap(lambda own, number: assign_block(jax.random.fold_in(arg_keys[8], 2), own, number, N_EXP * SEQ_DEV, EXPERTS, TOPK, CAPE, 2))(expert_ids_keys, expert_ids_turns).reshape((STEPS, BATCH, TOPK))
    gate_scores = set_ends(jax.random.randint(arg_keys[9], (STEPS, BATCH, TOPK), 1, 1001), jax.random.fold_in(arg_keys[9], 1), 1, 1000).astype(jnp.int32)
    gate_weight = scatter_about(arg_keys[10], (EXPERTS, FF, D), D ** -0.5, 0.09375, ((0, 16), (1, 2)))
    up_weight = scatter_about(arg_keys[11], (EXPERTS, FF, D), D ** -0.5, 0.09375, ((0, 16), (1, 2)))
    down_weight = scatter_about(arg_keys[12], (EXPERTS, FF, D), FF ** -0.5, 0.15625, ((0, 16), (1, 2)))
    return dict(residual=residual, queries=queries, key_cache=key_cache, value_cache=value_cache, new_keys=new_keys, new_values=new_values, cache_len=cache_len, norm_gain=norm_gain, expert_ids=expert_ids, gate_scores=gate_scores, gate_weight=gate_weight, up_weight=up_weight, down_weight=down_weight)


def attend_row(operands, step):
    head_query, keys_old, values_old, keys_new, values_new, length = operands
    group_size = QH // KVH
    scaling = 1.0 / math.sqrt(HD)
    joined_key_rows = jnp.concatenate([keys_old, keys_new], axis=0).astype(jnp.float32).reshape(CACHE + STEPS, KVH, HD)
    all_values = jnp.concatenate([values_old, values_new], axis=0).astype(jnp.float32).reshape(CACHE + STEPS, KVH, HD)
    query_heads = head_query.astype(jnp.float32).reshape(KVH, group_size, HD)
    scores = jnp.einsum('jgd,tjd->jgt', query_heads, joined_key_rows) * scaling
    position = jnp.arange(CACHE + STEPS, dtype=jnp.int32)
    valid = jnp.where(position < CACHE, position < length, position - CACHE <= step)
    scores = jnp.where(valid[None, None, :], scores, -1e+30)
    row_max = lax.optimization_barrier(jnp.max(scores, axis=-1, keepdims=True))
    expo = jnp.exp(scores - row_max)
    probs = (expo / lax.optimization_barrier(jnp.sum(expo, axis=-1, keepdims=True))).astype(jnp.bfloat16)
    blended = jnp.einsum('jgt,tjd->jgd', probs.astype(jnp.float32), all_values)
    return blended.reshape(QH * HD)

def norm_rows(hidden, norm_gain):
    mean_square = lax.optimization_barrier(jnp.mean(hidden * hidden, axis=-1, keepdims=True))
    return (hidden * lax.rsqrt(mean_square + 1e-06) * norm_gain.astype(jnp.float32)).astype(jnp.bfloat16)

def slot_targets(chosen, experts):
    flat_ids = chosen.reshape(-1)
    matches = (flat_ids[:, None] == jnp.arange(experts, dtype=jnp.int32)[None, :]).astype(jnp.int32)
    ranking = jnp.cumsum(matches, axis=0) - 1
    slot_rank = lax.optimization_barrier(jnp.sum(matches * ranking, axis=1))
    return (flat_ids * CAPE + slot_rank).reshape(chosen.shape)

def run_expert(operands, normed):
    row_index, gate_w, up_w, down_w = operands
    picked_rows = jnp.where((row_index > 0)[:, None], normed[jnp.maximum(row_index - 1, 0)], jnp.zeros((), jnp.bfloat16))
    gate_act = jnp.dot(picked_rows, gate_w.T, preferred_element_type=jnp.float32)
    up_act = jnp.dot(picked_rows, up_w.T, preferred_element_type=jnp.float32)
    hidden_activation = (jax.nn.silu(gate_act) * up_act).astype(jnp.bfloat16)
    unit_groups = hidden_activation.reshape(-1, N_EXP, FF // N_EXP).astype(jnp.float32)
    down_groups = down_w.reshape(N_EXP, FF // N_EXP, D).astype(jnp.float32)
    partial_value = jnp.einsum('rnf,nfd->rnd', unit_groups, down_groups)
    partial_value = lax.optimization_barrier(partial_value.astype(jnp.bfloat16)).astype(jnp.float32)
    return lax.optimization_barrier(jnp.sum(partial_value, axis=1))

def expert_mix(normed, chosen, gate_values, gate_weight, up_weight, down_weight):
    group_rows = N_EXP * SEQ_DEV
    grouped = chosen.reshape(N_REP, group_rows, TOPK)
    target = jax.vmap(lambda piece: slot_targets(piece, EXPERTS))(grouped)
    group_of = jnp.arange(N_REP, dtype=jnp.int32)[:, None, None]
    expert_of = target // CAPE
    slot_of = target % CAPE
    position_flat = (expert_of * N_REP + group_of) * CAPE + slot_of
    row_of = jnp.broadcast_to(jnp.arange(BATCH, dtype=jnp.int32).reshape(N_REP, group_rows, 1), position_flat.shape)
    table = jnp.zeros((EXPERTS * N_REP * CAPE,), jnp.int32).at[position_flat.reshape(-1)].set(row_of.reshape(-1) + 1)
    table = table.reshape(EXPERTS, N_REP * CAPE)
    outputs = lax.map(lambda operands: run_expert(operands, normed), (table, gate_weight, up_weight, down_weight))
    outputs = outputs.reshape(EXPERTS * N_REP * CAPE, D)
    selected_experts = jnp.take(outputs, position_flat.reshape(BATCH, TOPK), axis=0)
    return jnp.einsum('sv,svr->sr', gate_values, selected_experts)

def reference(residual, queries, key_cache, value_cache, new_keys, new_values, cache_len, norm_gain, expert_ids, gate_scores, gate_weight, up_weight, down_weight):
    keys_by_row = jnp.swapaxes(new_keys, 0, 1)
    values_by_row = jnp.swapaxes(new_values, 0, 1)
    results = []
    for step in range(STEPS):
        attention = lax.map(lambda operands: attend_row(operands, step), (queries[step], key_cache, value_cache, keys_by_row, values_by_row, cache_len))
        hidden = residual[step].astype(jnp.float32) + attention
        normed = norm_rows(hidden, norm_gain)
        unscaled_scores = gate_scores[step].astype(jnp.float32)
        gate_values = unscaled_scores / lax.optimization_barrier(jnp.sum(unscaled_scores, axis=-1, keepdims=True))
        expert_sum = expert_mix(normed, expert_ids[step], gate_values, gate_weight, up_weight, down_weight)
        results.append((hidden + expert_sum).astype(jnp.bfloat16))
    return jnp.stack(results)
```

```python
import math

import jax
import jax.numpy as jnp
from jax import lax
from jax.sharding import PartitionSpec as P

HD = 128


def attend_rows(queries, key_cache, value_cache, new_keys, new_values, cache_len):
    steps, rows, width = queries.shape
    cache = key_cache.shape[1]
    kv_heads = key_cache.shape[2] // HD
    group = width // HD // kv_heads
    scaling = 1.0 / math.sqrt(HD)
    heads = queries.reshape(steps, rows, kv_heads, group, HD).transpose(1, 2, 0, 3, 4)
    heads = heads.reshape(rows, kv_heads, steps * group, HD)
    keys = key_cache.reshape(rows, cache, kv_heads, HD)
    values = value_cache.reshape(rows, cache, kv_heads, HD)
    fresh_keys = new_keys.reshape(steps, rows, kv_heads, HD)
    fresh_values = new_values.reshape(steps, rows, kv_heads, HD)
    old = jnp.einsum("sjgd,stjd->sjgt", heads, keys, preferred_element_type=jnp.float32) * scaling
    new = (
        jnp.einsum("sjgd,tsjd->sjgt", heads, fresh_keys, preferred_element_type=jnp.float32)
        * scaling
    )
    position = lax.broadcasted_iota(jnp.int32, (1, 1, 1, cache), 3)
    old = jnp.where(position < cache_len[:, None, None, None], old, -1e30)
    step_of = lax.broadcasted_iota(jnp.int32, (1, 1, steps * group, steps), 2) // group
    fresh = lax.broadcasted_iota(jnp.int32, (1, 1, steps * group, steps), 3)
    new = jnp.where(fresh <= step_of, new, -1e30)
    top = jnp.maximum(
        jnp.max(old, axis=-1, keepdims=True), jnp.max(new, axis=-1, keepdims=True)
    )
    old, new = jnp.exp(old - top), jnp.exp(new - top)
    total = jnp.sum(old, axis=-1, keepdims=True) + jnp.sum(new, axis=-1, keepdims=True)
    old, new = (old / total).astype(jnp.bfloat16), (new / total).astype(jnp.bfloat16)
    out = jnp.einsum("sjgt,stjd->sjgd", old, values, preferred_element_type=jnp.float32)
    out = out + jnp.einsum(
        "sjgt,tsjd->sjgd", new, fresh_values, preferred_element_type=jnp.float32
    )
    out = out.reshape(rows, kv_heads, steps, group, HD).transpose(2, 0, 1, 3, 4)
    return out.reshape(steps, rows, width)


def norm_rows(hidden, norm_gain):
    mean_square = jnp.mean(hidden * hidden, axis=-1, keepdims=True)
    return (hidden * lax.rsqrt(mean_square + 1e-06) * norm_gain.astype(jnp.float32)).astype(
        jnp.bfloat16
    )


def per_device_plain(
    residual, queries, key_cache, value_cache, new_keys, new_values, cache_len, norm_gain,
    expert_ids, gate_scores, gate_weight, up_weight, down_weight,
):
    axes = ("rep", "exp")
    steps, rows, width = residual.shape
    local = gate_weight.shape[0]
    attention = attend_rows(queries, key_cache, value_cache, new_keys, new_values, cache_len)
    hidden = residual.astype(jnp.float32) + attention
    normed = norm_rows(hidden, norm_gain)
    scores = gate_scores.astype(jnp.float32)
    gates = scores / jnp.sum(scores, axis=-1, keepdims=True)
    tokens = lax.all_gather(normed.reshape(steps * rows, width), axes, axis=0, tiled=True)
    all_ids = lax.all_gather(expert_ids.reshape(steps * rows, -1), axes, axis=0, tiled=True)
    all_gates = lax.all_gather(gates.reshape(steps * rows, -1), axes, axis=0, tiled=True)
    mine = lax.axis_index("rep") * local + lax.broadcasted_iota(jnp.int32, (1, local, 1), 1)
    weight = jnp.sum(jnp.where(all_ids[:, None, :] == mine, all_gates[:, None, :], 0.0), axis=2)
    contract = (((1,), (1,)), ((), ()))
    units = gate_weight.shape[1]
    gate = lax.dot_general(
        tokens, gate_weight.reshape(local * units, width), contract,
        preferred_element_type=jnp.float32,
    )
    up = lax.dot_general(
        tokens, up_weight.reshape(local * units, width), contract,
        preferred_element_type=jnp.float32,
    )
    activation = (jax.nn.silu(gate) * up).reshape(-1, local, units) * weight[:, :, None]
    activation = activation.astype(jnp.bfloat16).reshape(-1, local * units)
    partial = jnp.dot(
        activation, down_weight.reshape(local * units, width), preferred_element_type=jnp.float32
    ).astype(jnp.bfloat16)
    mixed = lax.psum_scatter(partial, axes, scatter_dimension=0, tiled=True)
    mixed = mixed.reshape(steps, rows, width).astype(jnp.float32)
    return (hidden + mixed).astype(jnp.bfloat16)


def solution(mesh):
    in_specs = (
        P(None, ("rep", "exp"), None),
        P(None, ("rep", "exp"), None),
        P(("rep", "exp"), None, None),
        P(("rep", "exp"), None, None),
        P(None, ("rep", "exp"), None),
        P(None, ("rep", "exp"), None),
        P(("rep", "exp")),
        P(),
        P(None, ("rep", "exp"), None),
        P(None, ("rep", "exp"), None),
        P("rep", "exp", None),
        P("rep", "exp", None),
        P("rep", "exp", None),
    )
    out_specs = P(None, ("rep", "exp"), None)
    return jax.shard_map(
        per_device_plain, mesh=mesh, in_specs=in_specs, out_specs=out_specs, check_vma=False
    )
```

```python
import math

import jax
import jax.numpy as jnp
from jax import lax
from jax.experimental import pallas as pl
from jax.experimental.pallas import tpu as pltpu
from jax.sharding import PartitionSpec as P

HD = 128


def attend_rows(queries, key_cache, value_cache, new_keys, new_values, cache_len):
    steps, rows, width = queries.shape
    cache = key_cache.shape[1]
    kv_heads = key_cache.shape[2] // HD
    group = width // HD // kv_heads
    scaling = 1.0 / math.sqrt(HD)
    heads = queries.reshape(steps, rows, kv_heads, group, HD).transpose(1, 2, 0, 3, 4)
    heads = heads.reshape(rows, kv_heads, steps * group, HD)
    keys = key_cache.reshape(rows, cache, kv_heads, HD)
    values = value_cache.reshape(rows, cache, kv_heads, HD)
    fresh_keys = new_keys.reshape(steps, rows, kv_heads, HD)
    fresh_values = new_values.reshape(steps, rows, kv_heads, HD)
    old = jnp.einsum("sjgd,stjd->sjgt", heads, keys, preferred_element_type=jnp.float32) * scaling
    new = (
        jnp.einsum("sjgd,tsjd->sjgt", heads, fresh_keys, preferred_element_type=jnp.float32)
        * scaling
    )
    position = lax.broadcasted_iota(jnp.int32, (1, 1, 1, cache), 3)
    old = jnp.where(position < cache_len[:, None, None, None], old, -1e30)
    step_of = lax.broadcasted_iota(jnp.int32, (1, 1, steps * group, steps), 2) // group
    fresh = lax.broadcasted_iota(jnp.int32, (1, 1, steps * group, steps), 3)
    new = jnp.where(fresh <= step_of, new, -1e30)
    top = jnp.maximum(
        jnp.max(old, axis=-1, keepdims=True), jnp.max(new, axis=-1, keepdims=True)
    )
    old, new = jnp.exp(old - top), jnp.exp(new - top)
    total = jnp.sum(old, axis=-1, keepdims=True) + jnp.sum(new, axis=-1, keepdims=True)
    old, new = (old / total).astype(jnp.bfloat16), (new / total).astype(jnp.bfloat16)
    out = jnp.einsum("sjgt,stjd->sjgd", old, values, preferred_element_type=jnp.float32)
    out = out + jnp.einsum(
        "sjgt,tsjd->sjgd", new, fresh_values, preferred_element_type=jnp.float32
    )
    out = out.reshape(rows, kv_heads, steps, group, HD).transpose(2, 0, 1, 3, 4)
    return out.reshape(steps, rows, width)


def norm_rows(hidden, norm_gain):
    mean_square = jnp.mean(hidden * hidden, axis=-1, keepdims=True)
    return (hidden * lax.rsqrt(mean_square + 1e-06) * norm_gain.astype(jnp.float32)).astype(
        jnp.bfloat16
    )


def per_device_plain(
    residual, queries, key_cache, value_cache, new_keys, new_values, cache_len, norm_gain,
    expert_ids, gate_scores, gate_weight, up_weight, down_weight,
):
    axes = ("rep", "exp")
    steps, rows, width = residual.shape
    local = gate_weight.shape[0]
    attention = attend_rows(queries, key_cache, value_cache, new_keys, new_values, cache_len)
    hidden = residual.astype(jnp.float32) + attention
    normed = norm_rows(hidden, norm_gain)
    scores = gate_scores.astype(jnp.float32)
    gates = scores / jnp.sum(scores, axis=-1, keepdims=True)
    tokens = lax.all_gather(normed.reshape(steps * rows, width), axes, axis=0, tiled=True)
    all_ids = lax.all_gather(expert_ids.reshape(steps * rows, -1), axes, axis=0, tiled=True)
    all_gates = lax.all_gather(gates.reshape(steps * rows, -1), axes, axis=0, tiled=True)
    mine = lax.axis_index("rep") * local + lax.broadcasted_iota(jnp.int32, (1, local, 1), 1)
    weight = jnp.sum(jnp.where(all_ids[:, None, :] == mine, all_gates[:, None, :], 0.0), axis=2)
    contract = (((1,), (1,)), ((), ()))
    units = gate_weight.shape[1]
    gate = lax.dot_general(
        tokens, gate_weight.reshape(local * units, width), contract,
        preferred_element_type=jnp.float32,
    )
    up = lax.dot_general(
        tokens, up_weight.reshape(local * units, width), contract,
        preferred_element_type=jnp.float32,
    )
    activation = (jax.nn.silu(gate) * up).reshape(-1, local, units) * weight[:, :, None]
    activation = activation.astype(jnp.bfloat16).reshape(-1, local * units)
    partial = jnp.dot(
        activation, down_weight.reshape(local * units, width), preferred_element_type=jnp.float32
    ).astype(jnp.bfloat16)
    mixed = lax.psum_scatter(partial, axes, scatter_dimension=0, tiled=True)
    mixed = mixed.reshape(steps, rows, width).astype(jnp.float32)
    return (hidden + mixed).astype(jnp.bfloat16)


CHUNKS = 4
ROWS = 8
DEVICES = 32
MESH = pl.DeviceIdType.MESH
F32 = jnp.float32
BF16 = jnp.bfloat16
NT = (((1,), (1,)), ((), ()))


def attend_in_vmem(
    q_ref, k_ref, v_ref, nk_ref, nv_ref, len_ref, heads, fresh_k, fresh_v, att
):
    steps, seqs, width = q_ref.shape
    cache = k_ref.shape[1]
    kv_heads = k_ref.shape[2] // HD
    head_count = width // HD
    group = head_count // kv_heads
    scaling = 1.0 / math.sqrt(HD)
    for step in range(steps):
        rows = q_ref[step].astype(F32)
        for h in range(head_count):
            heads[step * seqs : (step + 1) * seqs, h, :] = rows[:, h * HD : (h + 1) * HD]
    fresh_k[...] = jnp.zeros_like(fresh_k)
    fresh_v[...] = jnp.zeros_like(fresh_v)
    for step in range(steps):
        key_rows = nk_ref[step].astype(F32)
        value_rows = nv_ref[step].astype(F32)
        for seq in range(seqs):
            for j in range(kv_heads):
                cols = slice(j * HD, (j + 1) * HD)
                at = seq * kv_heads + j
                fresh_k[at, step : step + 1, :] = key_rows[seq : seq + 1, cols]
                fresh_v[at, step : step + 1, :] = value_rows[seq : seq + 1, cols]
    total = steps * group
    position = lax.broadcasted_iota(jnp.int32, (total, cache), 1)
    fresh_at = lax.broadcasted_iota(jnp.int32, (total, HD), 1)
    step_of = lax.broadcasted_iota(jnp.int32, (total, HD), 0) // group
    for seq in range(seqs):
        valid = position < len_ref[seq]
        for j in range(kv_heads):
            at = seq * kv_heads + j
            cols = slice(j * HD, (j + 1) * HD)
            query = jnp.concatenate(
                [
                    heads[step * seqs + seq, j * group : (j + 1) * group, :]
                    for step in range(steps)
                ],
                axis=0,
            ).astype(BF16)
            old = lax.dot_general(query, k_ref[seq, :, cols], NT, preferred_element_type=F32)
            new = lax.dot_general(
                query, fresh_k[at].astype(BF16), NT, preferred_element_type=F32
            )
            old = jnp.where(valid, old * scaling, -1e30)
            new = jnp.where(fresh_at <= step_of, new * scaling, -1e30)
            top = jnp.maximum(
                jnp.max(old, axis=-1, keepdims=True), jnp.max(new, axis=-1, keepdims=True)
            )
            old, new = jnp.exp(old - top), jnp.exp(new - top)
            share = 1.0 / (
                jnp.sum(old, axis=-1, keepdims=True) + jnp.sum(new, axis=-1, keepdims=True)
            )
            old, new = (old * share).astype(BF16), (new * share).astype(BF16)
            out = jnp.dot(old, v_ref[seq, :, cols], preferred_element_type=F32)
            out = out + jnp.dot(new, fresh_v[at].astype(BF16), preferred_element_type=F32)
            for step in range(steps):
                att[step * seqs + seq, j * group : (j + 1) * group, :] = out[
                    step * group : (step + 1) * group
                ]


def layer_kernel(
    res_ref, q_ref, k_ref, v_ref, nk_ref, nv_ref, len_ref, gain_ref, ids_ref, score_ref,
    gate_hbm, up_hbm, down_hbm,
    out_ref,
    wg, wu, wd, heads, fresh_k, fresh_v, att, hid, own_gates, x, gates, xk, g_acc, u_acc, act,
    p, rc, r1, r2, rz, w_sem, ag_send, ag_recv, rs_send, rs_recv,
):
    steps, seqs, width = res_ref.shape
    local, units = gate_hbm.shape[0], gate_hbm.shape[1]
    cols = width // CHUNKS
    rep, y = lax.axis_index("rep"), lax.axis_index("exp")
    c = lax.rem(rep, 2)
    xx = lax.rem(lax.div(rep, 2), 2)
    z = lax.div(rep, 4)

    def device(z_at, x_at, c_at, y_at):
        return ((z_at * 2 + x_at) * 2 + c_at, y_at)

    def group(c_at, x_at, y_at):
        return ((c_at * 2 + x_at) * 2 + y_at) * 4

    px, py, pc = device(z, 1 - xx, c, y), device(z, xx, c, 1 - y), device(z, xx, 1 - c, y)
    zs = [lax.rem(z + dz, 4) for dz in range(4)]
    pz = [device(at, xx, c, y) for at in zs]
    mine = group(c, xx, y)
    me = mine + z

    weights = []
    for k in range(CHUNKS):
        at = pl.ds(k * cols, cols)
        weights.append(
            [
                pltpu.make_async_copy(gate_hbm.at[:, :, at], wg.at[k], w_sem.at[0, k]),
                pltpu.make_async_copy(up_hbm.at[:, :, at], wu.at[k], w_sem.at[1, k]),
            ]
        )
    downs = [
        pltpu.make_async_copy(
            down_hbm.at[:, :, pl.ds(k * cols, cols)], wd.at[k], w_sem.at[2, k]
        )
        for k in range(CHUNKS)
    ]
    for pair in weights:
        for copy in pair:
            copy.start()
    for copy in downs:
        copy.start()

    barrier = pltpu.get_barrier_semaphore()
    for peer in (px, py, pc, pz[1], pz[2], pz[3]):
        pl.semaphore_signal(barrier, inc=1, device_id=peer, device_id_type=MESH)

    attend_in_vmem(
        q_ref, k_ref, v_ref, nk_ref, nv_ref, len_ref, heads, fresh_k, fresh_v, att
    )
    hid[...] = jnp.zeros_like(hid)
    for h in range(width // HD):
        hid[0 : steps * seqs, h * HD : (h + 1) * HD] = att[:, h, :]
    for step in range(steps):
        at = slice(step * seqs, (step + 1) * seqs)
        hid[at, :] = hid[at, :] + res_ref[step].astype(F32)
    hidden = hid[...]
    mean_square = jnp.mean(hidden * hidden, axis=-1, keepdims=True)
    normed = (hidden * lax.rsqrt(mean_square + 1e-06) * gain_ref[...].astype(F32)).astype(BF16)
    for k in range(CHUNKS):
        x[k, me] = normed[:, k * cols : (k + 1) * cols]
    own_gates[...] = jnp.zeros_like(own_gates)
    lane = lax.broadcasted_iota(jnp.int32, (seqs, HD), 1)
    for step in range(steps):
        chosen = ids_ref[step]
        score = score_ref[step].astype(F32)
        score = score / jnp.sum(score, axis=-1, keepdims=True)
        spread = jnp.zeros((seqs, HD), F32)
        for place in range(chosen.shape[1]):
            spread = spread + jnp.where(
                lane == chosen[:, place : place + 1], score[:, place : place + 1], 0.0
            )
        own_gates[step * seqs : (step + 1) * seqs, :] = spread
    gates[me] = own_gates[...]

    started = []

    def send(src, dst, sems, i, j, peer):
        copy = pltpu.make_async_remote_copy(
            src_ref=src, dst_ref=dst, send_sem=sems[0].at[i, j], recv_sem=sems[1].at[i, j],
            device_id=peer, device_id_type=MESH,
        )
        copy.start()
        started.append(copy)

    def arrive(ref, sems, i, j, peer):
        pltpu.make_async_remote_copy(
            src_ref=ref, dst_ref=ref, send_sem=sems[0].at[i, j], recv_sem=sems[1].at[i, j],
            device_id=peer, device_id_type=MESH,
        ).wait_recv()

    ag, rs = (ag_send, ag_recv), (rs_send, rs_recv)
    pl.semaphore_wait(barrier, 6)

    parts = [x.at[0], gates] + [x.at[k] for k in range(1, CHUNKS)]
    own, side_x = pl.ds(mine, 4), pl.ds(group(c, 1 - xx, y), 4)
    side_y, corner = pl.ds(group(c, xx, 1 - y), 4), pl.ds(group(c, 1 - xx, 1 - y), 4)
    others = [
        pl.ds(group(1 - c, xx, y), 4), pl.ds(group(1 - c, 1 - xx, y), 4),
        pl.ds(group(1 - c, xx, 1 - y), 4), pl.ds(group(1 - c, 1 - xx, 1 - y), 4),
    ]

    def gather_z(i):
        for dz in (1, 2, 3):
            send(parts[i].at[me], parts[i].at[me], ag, i, dz, pz[dz])

    def gather_a(i):
        for dz in (1, 2, 3):
            back = lax.rem(z + 4 - dz, 4)
            arrive(parts[i].at[mine + back], ag, i, dz, pz[4 - dz])
        send(parts[i].at[own], parts[i].at[own], ag, i, 4, px)
        send(parts[i].at[own], parts[i].at[own], ag, i, 5, py)
        send(parts[i].at[own], parts[i].at[own], ag, i, 6, pc)

    def gather_b(i):
        arrive(parts[i].at[side_x], ag, i, 4, px)
        if i % 2 == 0:
            send(parts[i].at[side_x], parts[i].at[side_x], ag, i, 0, py)
        send(parts[i].at[side_x], parts[i].at[side_x], ag, i, 7, pc)
        arrive(parts[i].at[side_y], ag, i, 5, py)
        if i % 2 == 1:
            send(parts[i].at[side_y], parts[i].at[side_y], ag, i, 0, px)
        send(parts[i].at[side_y], parts[i].at[side_y], ag, i, 8, pc)

    def gather_c(i):
        arrive(parts[i].at[corner], ag, i, 0, py if i % 2 == 0 else px)
        send(parts[i].at[corner], parts[i].at[corner], ag, i, 9, pc)

    def gather_d(i):
        for n, at in enumerate(others):
            arrive(parts[i].at[at], ag, i, 6 + n, pc)

    def project(k):
        for copy in weights[k]:
            copy.wait()
        xk[...] = x[k].astype(F32).reshape(DEVICES * ROWS, cols).astype(BF16)

        @pl.loop(0, local)
        def _(e):
            tokens = xk[...]
            g = lax.dot_general(wg[k, e], tokens, NT, preferred_element_type=F32)
            u = lax.dot_general(wu[k, e], tokens, NT, preferred_element_type=F32)
            if k == 0:
                g_acc[e] = g
                u_acc[e] = u
            else:
                g_acc[e] += g
                u_acc[e] += u

    count = len(parts)
    for i in range(count):
        gather_z(i)
    for t in range(count + 3):
        if t < count:
            gather_a(t)
        if 0 <= t - 1 < count:
            gather_b(t - 1)
        if 0 <= t - 2 < count:
            gather_c(t - 2)
        if 0 <= t - 3 < count:
            i = t - 3
            gather_d(i)
            if i != 1:
                project(0 if i == 0 else i - 1)

    by_expert = gates[...].reshape(DEVICES * ROWS, HD).T
    row = lax.broadcasted_iota(jnp.int32, by_expert.shape, 0)
    tile = 256
    for e in range(local):
        gate_row = jnp.sum(
            jnp.where(row == rep * local + e, by_expert, 0.0), axis=0, keepdims=True
        )
        for n in range(units // tile):
            at = slice(n * tile, (n + 1) * tile)
            g, u = g_acc[e, at, :], u_acc[e, at, :]
            value = g / (1.0 + jnp.exp(-g)) * u * gate_row
            act[:, e * units + n * tile : e * units + (n + 1) * tile] = value.T.astype(BF16)

    half = cols // 2

    def reduce_0(n):
        downs[n].wait()

        for h in range(2):
            at = slice(h * half, (h + 1) * half)
            part = jnp.dot(act[:, 0:units], wd[n, 0, :, at], preferred_element_type=F32)
            for e in range(1, local):
                part = part + jnp.dot(
                    act[:, e * units : (e + 1) * units], wd[n, e, :, at],
                    preferred_element_type=F32,
                )
            p[n, :, :, at] = part.reshape(DEVICES, ROWS, half).astype(BF16)
        send(p.at[n, pl.ds((1 - c) * 16, 16)], rc.at[n], rs, n, 0, pc)

    def add(target, values):
        total = target[...].astype(F32)
        for value in values:
            total = total + value[...].astype(F32)
        target[...] = total.astype(BF16)

    def reduce_1(n):
        arrive(rc.at[n], rs, n, 0, pc)
        add(p.at[n, pl.ds(c * 16, 16)], [rc.at[n]])
        peer, near = (px, side_x) if n % 2 == 0 else (py, side_y)
        send(p.at[n, corner], r1.at[n, 0], rs, n, 1, peer)
        send(p.at[n, near], r1.at[n, 1], rs, n, 2, peer)

    def reduce_2(n):
        peer = px if n % 2 == 0 else py
        arrive(r1.at[n, 0], rs, n, 1, peer)
        onward, far = (py, side_y) if n % 2 == 0 else (px, side_x)
        add(p.at[n, far], [r1.at[n, 0]])
        send(p.at[n, far], r2.at[n], rs, n, 3, onward)

    def reduce_3(n):
        arrive(r1.at[n, 1], rs, n, 2, px if n % 2 == 0 else py)
        arrive(r2.at[n], rs, n, 3, py if n % 2 == 0 else px)
        add(p.at[n, own], [r1.at[n, 1], r2.at[n]])
        for dz in (1, 2, 3):
            send(p.at[n, mine + zs[dz]], rz.at[n, dz], rs, n, 3 + dz, pz[dz])

    def reduce_4(n):
        at = slice(n * cols, (n + 1) * cols)
        total = p[n, me].astype(F32)
        for dz in (1, 2, 3):
            arrive(rz.at[n, dz], rs, n, 3 + dz, pz[4 - dz])
            total = total + rz[n, dz].astype(F32)
        total = total + hid[:, at]
        for step in range(steps):
            out_ref[step, :, at] = total[step * seqs : (step + 1) * seqs].astype(BF16)

    stages = (reduce_0, reduce_1, reduce_2, reduce_3, reduce_4)
    for t in range(CHUNKS + len(stages) - 1):
        for lag, stage in enumerate(stages):
            if 0 <= t - lag < CHUNKS:
                stage(t - lag)
    for copy in started:
        copy.wait_send()


def per_device_kernel(
    residual, queries, key_cache, value_cache, new_keys, new_values, cache_len, norm_gain,
    expert_ids, gate_scores, gate_weight, up_weight, down_weight,
):
    steps, seqs, width = residual.shape
    local, units, _ = gate_weight.shape
    cols = width // CHUNKS
    kv_heads = key_cache.shape[2] // HD
    heads = width // HD
    vmem = pl.BlockSpec(memory_space=pltpu.VMEM)
    hbm = pl.BlockSpec(memory_space=pl.ANY)
    smem = pl.BlockSpec(memory_space=pltpu.SMEM)
    rows = DEVICES * ROWS
    return pl.pallas_call(
        layer_kernel,
        out_shape=jax.ShapeDtypeStruct(residual.shape, BF16),
        in_specs=[vmem] * 6 + [smem] + [vmem] * 3 + [hbm] * 3,
        out_specs=vmem,
        scratch_shapes=[
            pltpu.VMEM((CHUNKS, local, units, cols), BF16),
            pltpu.VMEM((CHUNKS, local, units, cols), BF16),
            pltpu.VMEM((CHUNKS, local, units, cols), BF16),
            pltpu.VMEM((steps * seqs, heads, HD), F32),
            pltpu.VMEM((seqs * kv_heads, HD, HD), F32),
            pltpu.VMEM((seqs * kv_heads, HD, HD), F32),
            pltpu.VMEM((steps * seqs, heads, HD), F32),
            pltpu.VMEM((ROWS, width), F32),
            pltpu.VMEM((ROWS, HD), F32),
            pltpu.VMEM((CHUNKS, DEVICES, ROWS, cols), BF16),
            pltpu.VMEM((DEVICES, ROWS, HD), F32),
            pltpu.VMEM((rows, cols), BF16),
            pltpu.VMEM((local, units, rows), F32),
            pltpu.VMEM((local, units, rows), F32),
            pltpu.VMEM((rows, local * units), BF16),
            pltpu.VMEM((CHUNKS, DEVICES, ROWS, cols), BF16),
            pltpu.VMEM((CHUNKS, 16, ROWS, cols), BF16),
            pltpu.VMEM((CHUNKS, 2, 4, ROWS, cols), BF16),
            pltpu.VMEM((CHUNKS, 4, ROWS, cols), BF16),
            pltpu.VMEM((CHUNKS, 4, ROWS, cols), BF16),
            pltpu.SemaphoreType.DMA((3, CHUNKS)),
            pltpu.SemaphoreType.DMA((CHUNKS + 1, 10)),
            pltpu.SemaphoreType.DMA((CHUNKS + 1, 10)),
            pltpu.SemaphoreType.DMA((CHUNKS, 7)),
            pltpu.SemaphoreType.DMA((CHUNKS, 7)),
        ],
        compiler_params=pltpu.CompilerParams(
            collective_id=0, has_side_effects=True, vmem_limit_bytes=60 * 1024 * 1024
        ),
    )(
        residual, queries, key_cache, value_cache, new_keys, new_values, cache_len,
        norm_gain.reshape(1, width), expert_ids, gate_scores, gate_weight, up_weight,
        down_weight,
    )


def solution(mesh):
    in_specs = (
        P(None, ("rep", "exp"), None),
        P(None, ("rep", "exp"), None),
        P(("rep", "exp"), None, None),
        P(("rep", "exp"), None, None),
        P(None, ("rep", "exp"), None),
        P(None, ("rep", "exp"), None),
        P(("rep", "exp")),
        P(),
        P(None, ("rep", "exp"), None),
        P(None, ("rep", "exp"), None),
        P("rep", "exp", None),
        P("rep", "exp", None),
        P("rep", "exp", None),
    )
    out_specs = P(None, ("rep", "exp"), None)
    fits = mesh.shape["rep"] == 16 and mesh.shape["exp"] == 2
    per_device = per_device_kernel if fits else per_device_plain
    return jax.shard_map(
        per_device, mesh=mesh, in_specs=in_specs, out_specs=out_specs, check_vma=False
    )
```

```python
import math

import jax
import jax.numpy as jnp
from jax import lax
from jax.experimental import pallas as pl
from jax.experimental.pallas import tpu as pltpu
from jax.sharding import PartitionSpec as P

HD = 128


def attend_rows(queries, key_cache, value_cache, new_keys, new_values, cache_len):
    steps, rows, width = queries.shape
    cache = key_cache.shape[1]
    kv_heads = key_cache.shape[2] // HD
    group = width // HD // kv_heads
    scaling = 1.0 / math.sqrt(HD)
    heads = queries.reshape(steps, rows, kv_heads, group, HD).transpose(1, 2, 0, 3, 4)
    heads = heads.reshape(rows, kv_heads, steps * group, HD)
    keys = key_cache.reshape(rows, cache, kv_heads, HD)
    values = value_cache.reshape(rows, cache, kv_heads, HD)
    fresh_keys = new_keys.reshape(steps, rows, kv_heads, HD)
    fresh_values = new_values.reshape(steps, rows, kv_heads, HD)
    old = jnp.einsum("sjgd,stjd->sjgt", heads, keys, preferred_element_type=jnp.float32) * scaling
    new = (
        jnp.einsum("sjgd,tsjd->sjgt", heads, fresh_keys, preferred_element_type=jnp.float32)
        * scaling
    )
    position = lax.broadcasted_iota(jnp.int32, (1, 1, 1, cache), 3)
    old = jnp.where(position < cache_len[:, None, None, None], old, -1e30)
    step_of = lax.broadcasted_iota(jnp.int32, (1, 1, steps * group, steps), 2) // group
    fresh = lax.broadcasted_iota(jnp.int32, (1, 1, steps * group, steps), 3)
    new = jnp.where(fresh <= step_of, new, -1e30)
    top = jnp.maximum(
        jnp.max(old, axis=-1, keepdims=True), jnp.max(new, axis=-1, keepdims=True)
    )
    old, new = jnp.exp(old - top), jnp.exp(new - top)
    total = jnp.sum(old, axis=-1, keepdims=True) + jnp.sum(new, axis=-1, keepdims=True)
    old, new = (old / total).astype(jnp.bfloat16), (new / total).astype(jnp.bfloat16)
    out = jnp.einsum("sjgt,stjd->sjgd", old, values, preferred_element_type=jnp.float32)
    out = out + jnp.einsum(
        "sjgt,tsjd->sjgd", new, fresh_values, preferred_element_type=jnp.float32
    )
    out = out.reshape(rows, kv_heads, steps, group, HD).transpose(2, 0, 1, 3, 4)
    return out.reshape(steps, rows, width)


def norm_rows(hidden, norm_gain):
    mean_square = jnp.mean(hidden * hidden, axis=-1, keepdims=True)
    return (hidden * lax.rsqrt(mean_square + 1e-06) * norm_gain.astype(jnp.float32)).astype(
        jnp.bfloat16
    )


def per_device_plain(
    residual, queries, key_cache, value_cache, new_keys, new_values, cache_len, norm_gain,
    expert_ids, gate_scores, gate_weight, up_weight, down_weight,
):
    axes = ("rep", "exp")
    steps, rows, width = residual.shape
    local = gate_weight.shape[0]
    attention = attend_rows(queries, key_cache, value_cache, new_keys, new_values, cache_len)
    hidden = residual.astype(jnp.float32) + attention
    normed = norm_rows(hidden, norm_gain)
    scores = gate_scores.astype(jnp.float32)
    gates = scores / jnp.sum(scores, axis=-1, keepdims=True)
    tokens = lax.all_gather(normed.reshape(steps * rows, width), axes, axis=0, tiled=True)
    all_ids = lax.all_gather(expert_ids.reshape(steps * rows, -1), axes, axis=0, tiled=True)
    all_gates = lax.all_gather(gates.reshape(steps * rows, -1), axes, axis=0, tiled=True)
    mine = lax.axis_index("rep") * local + lax.broadcasted_iota(jnp.int32, (1, local, 1), 1)
    weight = jnp.sum(jnp.where(all_ids[:, None, :] == mine, all_gates[:, None, :], 0.0), axis=2)
    contract = (((1,), (1,)), ((), ()))
    units = gate_weight.shape[1]
    gate = lax.dot_general(
        tokens, gate_weight.reshape(local * units, width), contract,
        preferred_element_type=jnp.float32,
    )
    up = lax.dot_general(
        tokens, up_weight.reshape(local * units, width), contract,
        preferred_element_type=jnp.float32,
    )
    activation = (jax.nn.silu(gate) * up).reshape(-1, local, units) * weight[:, :, None]
    activation = activation.astype(jnp.bfloat16).reshape(-1, local * units)
    partial = jnp.dot(
        activation, down_weight.reshape(local * units, width), preferred_element_type=jnp.float32
    ).astype(jnp.bfloat16)
    mixed = lax.psum_scatter(partial, axes, scatter_dimension=0, tiled=True)
    mixed = mixed.reshape(steps, rows, width).astype(jnp.float32)
    return (hidden + mixed).astype(jnp.bfloat16)


CHUNKS = 4
ROWS = 8
DEVICES = 32
MESH = pl.DeviceIdType.MESH
F32 = jnp.float32
BF16 = jnp.bfloat16
NT = (((1,), (1,)), ((), ()))


def attend_in_vmem(
    q_ref, k_ref, v_ref, nk_ref, nv_ref, len_ref, heads, fresh_k, fresh_v, att
):
    steps, seqs, width = q_ref.shape
    cache = k_ref.shape[1]
    kv_heads = k_ref.shape[2] // HD
    head_count = width // HD
    group = head_count // kv_heads
    scaling = 1.0 / math.sqrt(HD)
    for step in range(steps):
        rows = q_ref[step].astype(F32)
        for h in range(head_count):
            heads[step * seqs : (step + 1) * seqs, h, :] = rows[:, h * HD : (h + 1) * HD]
    fresh_k[...] = jnp.zeros_like(fresh_k)
    fresh_v[...] = jnp.zeros_like(fresh_v)
    for step in range(steps):
        key_rows = nk_ref[step].astype(F32)
        value_rows = nv_ref[step].astype(F32)
        for seq in range(seqs):
            for j in range(kv_heads):
                cols = slice(j * HD, (j + 1) * HD)
                at = seq * kv_heads + j
                fresh_k[at, step : step + 1, :] = key_rows[seq : seq + 1, cols]
                fresh_v[at, step : step + 1, :] = value_rows[seq : seq + 1, cols]
    total = steps * group
    position = lax.broadcasted_iota(jnp.int32, (total, cache), 1)
    fresh_at = lax.broadcasted_iota(jnp.int32, (total, HD), 1)
    step_of = lax.broadcasted_iota(jnp.int32, (total, HD), 0) // group
    for seq in range(seqs):
        valid = position < len_ref[seq]
        for j in range(kv_heads):
            at = seq * kv_heads + j
            cols = slice(j * HD, (j + 1) * HD)
            query = jnp.concatenate(
                [
                    heads[step * seqs + seq, j * group : (j + 1) * group, :]
                    for step in range(steps)
                ],
                axis=0,
            ).astype(BF16)
            old = lax.dot_general(query, k_ref[seq, :, cols], NT, preferred_element_type=F32)
            new = lax.dot_general(
                query, fresh_k[at].astype(BF16), NT, preferred_element_type=F32
            )
            old = jnp.where(valid, old * scaling, -1e30)
            new = jnp.where(fresh_at <= step_of, new * scaling, -1e30)
            top = jnp.maximum(
                jnp.max(old, axis=-1, keepdims=True), jnp.max(new, axis=-1, keepdims=True)
            )
            old, new = jnp.exp(old - top), jnp.exp(new - top)
            share = 1.0 / (
                jnp.sum(old, axis=-1, keepdims=True) + jnp.sum(new, axis=-1, keepdims=True)
            )
            old, new = (old * share).astype(BF16), (new * share).astype(BF16)
            out = jnp.dot(old, v_ref[seq, :, cols], preferred_element_type=F32)
            out = out + jnp.dot(new, fresh_v[at].astype(BF16), preferred_element_type=F32)
            for step in range(steps):
                att[step * seqs + seq, j * group : (j + 1) * group, :] = out[
                    step * group : (step + 1) * group
                ]


def layer_kernel(
    res_ref, q_ref, k_ref, v_ref, nk_ref, nv_ref, len_ref, gain_ref, ids_ref, score_ref,
    gate_hbm, up_hbm, down_hbm,
    out_ref,
    wg, wu, wd, heads, fresh_k, fresh_v, att, hid, own_gates, x, gates, xk, g_acc, u_acc, act,
    p, rc, r1, r2, rz, w_sem, ag_send, ag_recv, rs_send, rs_recv,
):
    steps, seqs, width = res_ref.shape
    local, units = gate_hbm.shape[0], gate_hbm.shape[1]
    cols = width // CHUNKS
    rep, y = lax.axis_index("rep"), lax.axis_index("exp")
    c = lax.rem(rep, 2)
    xx = lax.rem(lax.div(rep, 2), 2)
    z = lax.div(rep, 4)

    def device(z_at, x_at, c_at, y_at):
        return ((z_at * 2 + x_at) * 2 + c_at, y_at)

    def group(c_at, x_at, y_at):
        return ((c_at * 2 + x_at) * 2 + y_at) * 4

    px, py, pc = device(z, 1 - xx, c, y), device(z, xx, c, 1 - y), device(z, xx, 1 - c, y)
    zs = [lax.rem(z + dz, 4) for dz in range(4)]
    pz = [device(at, xx, c, y) for at in zs]
    mine = group(c, xx, y)
    me = mine + z

    weights = []
    for k in range(CHUNKS):
        at = pl.ds(k * cols, cols)
        weights.append(
            [
                pltpu.make_async_copy(gate_hbm.at[:, :, at], wg.at[k], w_sem.at[0, k]),
                pltpu.make_async_copy(up_hbm.at[:, :, at], wu.at[k], w_sem.at[1, k]),
            ]
        )
    downs = [
        pltpu.make_async_copy(
            down_hbm.at[:, :, pl.ds(k * cols, cols)], wd.at[k], w_sem.at[2, k]
        )
        for k in range(CHUNKS)
    ]
    for pair in weights:
        for copy in pair:
            copy.start()
    for copy in downs:
        copy.start()

    barrier = pltpu.get_barrier_semaphore()
    for peer in (px, py, pc, pz[1], pz[2], pz[3]):
        pl.semaphore_signal(barrier, inc=1, device_id=peer, device_id_type=MESH)

    attend_in_vmem(
        q_ref, k_ref, v_ref, nk_ref, nv_ref, len_ref, heads, fresh_k, fresh_v, att
    )
    hid[...] = jnp.zeros_like(hid)
    for h in range(width // HD):
        hid[0 : steps * seqs, h * HD : (h + 1) * HD] = att[:, h, :]
    for step in range(steps):
        at = slice(step * seqs, (step + 1) * seqs)
        hid[at, :] = hid[at, :] + res_ref[step].astype(F32)
    hidden = hid[...]
    mean_square = jnp.mean(hidden * hidden, axis=-1, keepdims=True)
    normed = (hidden * lax.rsqrt(mean_square + 1e-06) * gain_ref[...].astype(F32).reshape(1, width)).astype(
        BF16
    )
    for k in range(CHUNKS):
        x[k, me] = normed[:, k * cols : (k + 1) * cols]
    own_gates[...] = jnp.zeros_like(own_gates)
    lane = lax.broadcasted_iota(jnp.int32, (seqs, HD), 1)
    for step in range(steps):
        chosen = ids_ref[step]
        score = score_ref[step].astype(F32)
        score = score / jnp.sum(score, axis=-1, keepdims=True)
        spread = jnp.zeros((seqs, HD), F32)
        for place in range(chosen.shape[1]):
            spread = spread + jnp.where(
                lane == chosen[:, place : place + 1], score[:, place : place + 1], 0.0
            )
        own_gates[step * seqs : (step + 1) * seqs, :] = spread
    gates[me] = own_gates[...]

    started = []

    def send(src, dst, sems, i, j, peer):
        copy = pltpu.make_async_remote_copy(
            src_ref=src, dst_ref=dst, send_sem=sems[0].at[i, j], recv_sem=sems[1].at[i, j],
            device_id=peer, device_id_type=MESH,
        )
        copy.start()
        started.append(copy)

    def arrive(ref, sems, i, j, peer):
        pltpu.make_async_remote_copy(
            src_ref=ref, dst_ref=ref, send_sem=sems[0].at[i, j], recv_sem=sems[1].at[i, j],
            device_id=peer, device_id_type=MESH,
        ).wait_recv()

    ag, rs = (ag_send, ag_recv), (rs_send, rs_recv)
    pl.semaphore_wait(barrier, 6)

    parts = [x.at[k] for k in range(CHUNKS)] + [gates]
    own, side_x = pl.ds(mine, 4), pl.ds(group(c, 1 - xx, y), 4)
    side_y, corner = pl.ds(group(c, xx, 1 - y), 4), pl.ds(group(c, 1 - xx, 1 - y), 4)
    others = [
        pl.ds(group(1 - c, xx, y), 4), pl.ds(group(1 - c, 1 - xx, y), 4),
        pl.ds(group(1 - c, xx, 1 - y), 4), pl.ds(group(1 - c, 1 - xx, 1 - y), 4),
    ]

    def gather_z(i):
        for dz in (1, 2, 3):
            send(parts[i].at[me], parts[i].at[me], ag, i, dz, pz[dz])

    def gather_a(i):
        for dz in (1, 2, 3):
            back = lax.rem(z + 4 - dz, 4)
            arrive(parts[i].at[mine + back], ag, i, dz, pz[4 - dz])
        send(parts[i].at[own], parts[i].at[own], ag, i, 4, px)
        send(parts[i].at[own], parts[i].at[own], ag, i, 5, py)
        send(parts[i].at[own], parts[i].at[own], ag, i, 6, pc)

    def gather_b(i):
        arrive(parts[i].at[side_x], ag, i, 4, px)
        if i % 2 == 0:
            send(parts[i].at[side_x], parts[i].at[side_x], ag, i, 0, py)
        send(parts[i].at[side_x], parts[i].at[side_x], ag, i, 7, pc)
        arrive(parts[i].at[side_y], ag, i, 5, py)
        if i % 2 == 1:
            send(parts[i].at[side_y], parts[i].at[side_y], ag, i, 0, px)
        send(parts[i].at[side_y], parts[i].at[side_y], ag, i, 8, pc)

    def gather_c(i):
        arrive(parts[i].at[corner], ag, i, 0, py if i % 2 == 0 else px)
        send(parts[i].at[corner], parts[i].at[corner], ag, i, 9, pc)

    def gather_d(i):
        for n, at in enumerate(others):
            arrive(parts[i].at[at], ag, i, 6 + n, pc)

    def project(k):
        for copy in weights[k]:
            copy.wait()
        xk[...] = x[k].astype(F32).reshape(DEVICES * ROWS, cols).astype(BF16)

        @pl.loop(0, local)
        def _(e):
            tokens = xk[...]
            g = lax.dot_general(wg[k, e], tokens, NT, preferred_element_type=F32)
            u = lax.dot_general(wu[k, e], tokens, NT, preferred_element_type=F32)
            if k == 0:
                g_acc[e] = g
                u_acc[e] = u
            else:
                g_acc[e] += g
                u_acc[e] += u

    def project_last(k):
        for copy in weights[k]:
            copy.wait()
        xk[...] = x[k].astype(F32).reshape(DEVICES * ROWS, cols).astype(BF16)
        by_expert = gates[...].reshape(DEVICES * ROWS, HD).T
        row = lax.broadcasted_iota(jnp.int32, by_expert.shape, 0)
        tokens = xk[...]
        tile = 256
        for e in range(local):
            gate_row = jnp.sum(
                jnp.where(row == rep * local + e, by_expert, 0.0), axis=0, keepdims=True
            )
            g_all = lax.dot_general(wg[k, e], tokens, NT, preferred_element_type=F32)
            u_all = lax.dot_general(wu[k, e], tokens, NT, preferred_element_type=F32)
            for n in range(units // tile):
                at = slice(n * tile, (n + 1) * tile)
                g, u = g_acc[e, at, :] + g_all[at], u_acc[e, at, :] + u_all[at]
                value = g / (1.0 + jnp.exp(-g)) * u * gate_row
                first = e * units + n * tile
                act[:, first : first + tile] = value.T.astype(BF16)

    turns = [[0, CHUNKS]] + [[k] for k in range(1, CHUNKS)]
    for i in turns[0]:
        gather_z(i)
    for t in range(CHUNKS + 3):
        if t + 1 < CHUNKS:
            for i in turns[t + 1]:
                gather_z(i)
        for lag, stage in enumerate((gather_a, gather_b, gather_c, gather_d)):
            if 0 <= t - lag < CHUNKS:
                for i in turns[t - lag]:
                    stage(i)
        if 0 <= t - 3 < CHUNKS - 1:
            project(t - 3)
    project_last(CHUNKS - 1)

    half = cols // 2

    def reduce_0(n):
        downs[n].wait()

        for h in range(2):
            at = slice(h * half, (h + 1) * half)
            part = jnp.dot(act[:, 0:units], wd[n, 0, :, at], preferred_element_type=F32)
            for e in range(1, local):
                part = part + jnp.dot(
                    act[:, e * units : (e + 1) * units], wd[n, e, :, at],
                    preferred_element_type=F32,
                )
            p[n, :, :, at] = part.reshape(DEVICES, ROWS, half).astype(BF16)
        send(p.at[n, pl.ds((1 - c) * 16, 16)], rc.at[n], rs, n, 0, pc)

    def add(target, values):
        total = target[...].astype(F32)
        for value in values:
            total = total + value[...].astype(F32)
        target[...] = total.astype(BF16)

    def reduce_1(n):
        arrive(rc.at[n], rs, n, 0, pc)
        add(p.at[n, pl.ds(c * 16, 16)], [rc.at[n]])
        peer, near = (px, side_x) if n % 2 == 0 else (py, side_y)
        send(p.at[n, corner], r1.at[n, 0], rs, n, 1, peer)
        send(p.at[n, near], r1.at[n, 1], rs, n, 2, peer)

    def reduce_2(n):
        peer = px if n % 2 == 0 else py
        arrive(r1.at[n, 0], rs, n, 1, peer)
        onward, far = (py, side_y) if n % 2 == 0 else (px, side_x)
        add(p.at[n, far], [r1.at[n, 0]])
        send(p.at[n, far], r2.at[n], rs, n, 3, onward)

    def reduce_3(n):
        arrive(r1.at[n, 1], rs, n, 2, px if n % 2 == 0 else py)
        arrive(r2.at[n], rs, n, 3, py if n % 2 == 0 else px)
        add(p.at[n, own], [r1.at[n, 1], r2.at[n]])
        for dz in (1, 2, 3):
            send(p.at[n, mine + zs[dz]], rz.at[n, dz], rs, n, 3 + dz, pz[dz])

    def reduce_4(n):
        at = slice(n * cols, (n + 1) * cols)
        total = p[n, me].astype(F32)
        for dz in (1, 2, 3):
            arrive(rz.at[n, dz], rs, n, 3 + dz, pz[4 - dz])
            total = total + rz[n, dz].astype(F32)
        total = total + hid[:, at]
        for step in range(steps):
            out_ref[step, :, at] = total[step * seqs : (step + 1) * seqs].astype(BF16)

    stages = (reduce_0, reduce_1, reduce_2, reduce_3, reduce_4)
    for t in range(CHUNKS + len(stages) - 1):
        for lag, stage in enumerate(stages):
            if 0 <= t - lag < CHUNKS:
                stage(t - lag)
    for copy in started:
        copy.wait_send()


def per_device_kernel(
    residual, queries, key_cache, value_cache, new_keys, new_values, cache_len, norm_gain,
    expert_ids, gate_scores, gate_weight, up_weight, down_weight,
):
    steps, seqs, width = residual.shape
    local, units, _ = gate_weight.shape
    cols = width // CHUNKS
    kv_heads = key_cache.shape[2] // HD
    heads = width // HD
    vmem = pl.BlockSpec(memory_space=pltpu.VMEM)
    hbm = pl.BlockSpec(memory_space=pl.ANY)
    smem = pl.BlockSpec(memory_space=pltpu.SMEM)
    rows = DEVICES * ROWS
    return pl.pallas_call(
        layer_kernel,
        out_shape=jax.ShapeDtypeStruct(residual.shape, BF16),
        in_specs=[vmem] * 6 + [smem] + [vmem] * 3 + [hbm] * 3,
        out_specs=vmem,
        scratch_shapes=[
            pltpu.VMEM((CHUNKS, local, units, cols), BF16),
            pltpu.VMEM((CHUNKS, local, units, cols), BF16),
            pltpu.VMEM((CHUNKS, local, units, cols), BF16),
            pltpu.VMEM((steps * seqs, heads, HD), F32),
            pltpu.VMEM((seqs * kv_heads, HD, HD), F32),
            pltpu.VMEM((seqs * kv_heads, HD, HD), F32),
            pltpu.VMEM((steps * seqs, heads, HD), F32),
            pltpu.VMEM((ROWS, width), F32),
            pltpu.VMEM((ROWS, HD), F32),
            pltpu.VMEM((CHUNKS, DEVICES, ROWS, cols), BF16),
            pltpu.VMEM((DEVICES, ROWS, HD), F32),
            pltpu.VMEM((rows, cols), BF16),
            pltpu.VMEM((local, units, rows), F32),
            pltpu.VMEM((local, units, rows), F32),
            pltpu.VMEM((rows, local * units), BF16),
            pltpu.VMEM((CHUNKS, DEVICES, ROWS, cols), BF16),
            pltpu.VMEM((CHUNKS, 16, ROWS, cols), BF16),
            pltpu.VMEM((CHUNKS, 2, 4, ROWS, cols), BF16),
            pltpu.VMEM((CHUNKS, 4, ROWS, cols), BF16),
            pltpu.VMEM((CHUNKS, 4, ROWS, cols), BF16),
            pltpu.SemaphoreType.DMA((3, CHUNKS)),
            pltpu.SemaphoreType.DMA((CHUNKS + 1, 10)),
            pltpu.SemaphoreType.DMA((CHUNKS + 1, 10)),
            pltpu.SemaphoreType.DMA((CHUNKS, 7)),
            pltpu.SemaphoreType.DMA((CHUNKS, 7)),
        ],
        compiler_params=pltpu.CompilerParams(
            collective_id=0, has_side_effects=True, vmem_limit_bytes=60 * 1024 * 1024
        ),
    )(
        residual, queries, key_cache, value_cache, new_keys, new_values, cache_len,
        norm_gain, expert_ids, gate_scores, gate_weight, up_weight,
        down_weight,
    )


def solution(mesh):
    in_specs = (
        P(None, ("rep", "exp"), None),
        P(None, ("rep", "exp"), None),
        P(("rep", "exp"), None, None),
        P(("rep", "exp"), None, None),
        P(None, ("rep", "exp"), None),
        P(None, ("rep", "exp"), None),
        P(("rep", "exp")),
        P(),
        P(None, ("rep", "exp"), None),
        P(None, ("rep", "exp"), None),
        P("rep", "exp", None),
        P("rep", "exp", None),
        P("rep", "exp", None),
    )
    out_specs = P(None, ("rep", "exp"), None)
    fits = mesh.shape["rep"] == 16 and mesh.shape["exp"] == 2
    per_device = per_device_kernel if fits else per_device_plain
    return jax.shard_map(
        per_device, mesh=mesh, in_specs=in_specs, out_specs=out_specs, check_vma=False
    )
```

```python
import math

import jax
import jax.numpy as jnp
from jax import lax
from jax.experimental import pallas as pl
from jax.experimental.pallas import tpu as pltpu
from jax.sharding import PartitionSpec as P

HD = 128


def attend_rows(queries, key_cache, value_cache, new_keys, new_values, cache_len):
    steps, rows, width = queries.shape
    cache = key_cache.shape[1]
    kv_heads = key_cache.shape[2] // HD
    group = width // HD // kv_heads
    scaling = 1.0 / math.sqrt(HD)
    heads = queries.reshape(steps, rows, kv_heads, group, HD).transpose(1, 2, 0, 3, 4)
    heads = heads.reshape(rows, kv_heads, steps * group, HD)
    keys = key_cache.reshape(rows, cache, kv_heads, HD)
    values = value_cache.reshape(rows, cache, kv_heads, HD)
    fresh_keys = new_keys.reshape(steps, rows, kv_heads, HD)
    fresh_values = new_values.reshape(steps, rows, kv_heads, HD)
    old = jnp.einsum("sjgd,stjd->sjgt", heads, keys, preferred_element_type=jnp.float32) * scaling
    new = (
        jnp.einsum("sjgd,tsjd->sjgt", heads, fresh_keys, preferred_element_type=jnp.float32)
        * scaling
    )
    position = lax.broadcasted_iota(jnp.int32, (1, 1, 1, cache), 3)
    old = jnp.where(position < cache_len[:, None, None, None], old, -1e30)
    step_of = lax.broadcasted_iota(jnp.int32, (1, 1, steps * group, steps), 2) // group
    fresh = lax.broadcasted_iota(jnp.int32, (1, 1, steps * group, steps), 3)
    new = jnp.where(fresh <= step_of, new, -1e30)
    top = jnp.maximum(
        jnp.max(old, axis=-1, keepdims=True), jnp.max(new, axis=-1, keepdims=True)
    )
    old, new = jnp.exp(old - top), jnp.exp(new - top)
    total = jnp.sum(old, axis=-1, keepdims=True) + jnp.sum(new, axis=-1, keepdims=True)
    old, new = (old / total).astype(jnp.bfloat16), (new / total).astype(jnp.bfloat16)
    out = jnp.einsum("sjgt,stjd->sjgd", old, values, preferred_element_type=jnp.float32)
    out = out + jnp.einsum(
        "sjgt,tsjd->sjgd", new, fresh_values, preferred_element_type=jnp.float32
    )
    out = out.reshape(rows, kv_heads, steps, group, HD).transpose(2, 0, 1, 3, 4)
    return out.reshape(steps, rows, width)


def norm_rows(hidden, norm_gain):
    mean_square = jnp.mean(hidden * hidden, axis=-1, keepdims=True)
    return (hidden * lax.rsqrt(mean_square + 1e-06) * norm_gain.astype(jnp.float32)).astype(
        jnp.bfloat16
    )


def per_device_plain(
    residual, queries, key_cache, value_cache, new_keys, new_values, cache_len, norm_gain,
    expert_ids, gate_scores, gate_weight, up_weight, down_weight,
):
    axes = ("rep", "exp")
    steps, rows, width = residual.shape
    local = gate_weight.shape[0]
    attention = attend_rows(queries, key_cache, value_cache, new_keys, new_values, cache_len)
    hidden = residual.astype(jnp.float32) + attention
    normed = norm_rows(hidden, norm_gain)
    scores = gate_scores.astype(jnp.float32)
    gates = scores / jnp.sum(scores, axis=-1, keepdims=True)
    tokens = lax.all_gather(normed.reshape(steps * rows, width), axes, axis=0, tiled=True)
    all_ids = lax.all_gather(expert_ids.reshape(steps * rows, -1), axes, axis=0, tiled=True)
    all_gates = lax.all_gather(gates.reshape(steps * rows, -1), axes, axis=0, tiled=True)
    mine = lax.axis_index("rep") * local + lax.broadcasted_iota(jnp.int32, (1, local, 1), 1)
    weight = jnp.sum(jnp.where(all_ids[:, None, :] == mine, all_gates[:, None, :], 0.0), axis=2)
    contract = (((1,), (1,)), ((), ()))
    units = gate_weight.shape[1]
    gate = lax.dot_general(
        tokens, gate_weight.reshape(local * units, width), contract,
        preferred_element_type=jnp.float32,
    )
    up = lax.dot_general(
        tokens, up_weight.reshape(local * units, width), contract,
        preferred_element_type=jnp.float32,
    )
    activation = (jax.nn.silu(gate) * up).reshape(-1, local, units) * weight[:, :, None]
    activation = activation.astype(jnp.bfloat16).reshape(-1, local * units)
    partial = jnp.dot(
        activation, down_weight.reshape(local * units, width), preferred_element_type=jnp.float32
    ).astype(jnp.bfloat16)
    mixed = lax.psum_scatter(partial, axes, scatter_dimension=0, tiled=True)
    mixed = mixed.reshape(steps, rows, width).astype(jnp.float32)
    return (hidden + mixed).astype(jnp.bfloat16)


CHUNKS = 4
ROWS = 8
DEVICES = 32
MESH = pl.DeviceIdType.MESH
F32 = jnp.float32
BF16 = jnp.bfloat16
NT = (((1,), (1,)), ((), ()))


def attend_in_vmem(
    q_ref, k_ref, v_ref, nk_ref, nv_ref, len_ref, heads, fresh_k, fresh_v, att
):
    steps, seqs, width = q_ref.shape
    cache = k_ref.shape[1]
    kv_heads = k_ref.shape[2] // HD
    head_count = width // HD
    group = head_count // kv_heads
    scaling = 1.0 / math.sqrt(HD)
    for step in range(steps):
        rows = q_ref[step].astype(F32)
        for h in range(head_count):
            heads[step * seqs : (step + 1) * seqs, h, :] = rows[:, h * HD : (h + 1) * HD]
    fresh_k[...] = jnp.zeros_like(fresh_k)
    fresh_v[...] = jnp.zeros_like(fresh_v)
    for step in range(steps):
        key_rows = nk_ref[step].astype(F32)
        value_rows = nv_ref[step].astype(F32)
        for seq in range(seqs):
            for j in range(kv_heads):
                cols = slice(j * HD, (j + 1) * HD)
                at = seq * kv_heads + j
                fresh_k[at, step : step + 1, :] = key_rows[seq : seq + 1, cols]
                fresh_v[at, step : step + 1, :] = value_rows[seq : seq + 1, cols]
    total = steps * group
    position = lax.broadcasted_iota(jnp.int32, (total, cache), 1)
    fresh_at = lax.broadcasted_iota(jnp.int32, (total, HD), 1)
    step_of = lax.broadcasted_iota(jnp.int32, (total, HD), 0) // group
    for seq in range(seqs):
        valid = position < len_ref[seq]
        for j in range(kv_heads):
            at = seq * kv_heads + j
            cols = slice(j * HD, (j + 1) * HD)
            query = jnp.concatenate(
                [
                    heads[step * seqs + seq, j * group : (j + 1) * group, :]
                    for step in range(steps)
                ],
                axis=0,
            ).astype(BF16)
            old = lax.dot_general(query, k_ref[seq, :, cols], NT, preferred_element_type=F32)
            new = lax.dot_general(
                query, fresh_k[at].astype(BF16), NT, preferred_element_type=F32
            )
            old = jnp.where(valid, old * scaling, -1e30)
            new = jnp.where(fresh_at <= step_of, new * scaling, -1e30)
            top = jnp.maximum(
                jnp.max(old, axis=-1, keepdims=True), jnp.max(new, axis=-1, keepdims=True)
            )
            old, new = jnp.exp(old - top), jnp.exp(new - top)
            share = 1.0 / (
                jnp.sum(old, axis=-1, keepdims=True) + jnp.sum(new, axis=-1, keepdims=True)
            )
            old, new = (old * share).astype(BF16), (new * share).astype(BF16)
            out = jnp.dot(old, v_ref[seq, :, cols], preferred_element_type=F32)
            out = out + jnp.dot(new, fresh_v[at].astype(BF16), preferred_element_type=F32)
            for step in range(steps):
                att[step * seqs + seq, j * group : (j + 1) * group, :] = out[
                    step * group : (step + 1) * group
                ]


def layer_kernel(
    res_ref, q_ref, k_ref, v_ref, nk_ref, nv_ref, len_ref, gain_ref, ids_ref, score_ref,
    gate_hbm, up_hbm, down_hbm,
    out_ref,
    wg, wu, wd, heads, fresh_k, fresh_v, att, hid, own_gates, x, gates, xk, g_acc, u_acc, act,
    p, rc, r1, r2, rz, w_sem, ag_send, ag_recv, rs_send, rs_recv,
):
    steps, seqs, width = res_ref.shape
    local, units = gate_hbm.shape[0], gate_hbm.shape[1]
    cols = width // CHUNKS
    rep, y = lax.axis_index("rep"), lax.axis_index("exp")
    c = lax.rem(rep, 2)
    xx = lax.rem(lax.div(rep, 2), 2)
    z = lax.div(rep, 4)

    def device(z_at, x_at, c_at, y_at):
        return ((z_at * 2 + x_at) * 2 + c_at, y_at)

    def group(c_at, x_at, y_at):
        return ((c_at * 2 + x_at) * 2 + y_at) * 4

    px, py, pc = device(z, 1 - xx, c, y), device(z, xx, c, 1 - y), device(z, xx, 1 - c, y)
    zs = [lax.rem(z + dz, 4) for dz in range(4)]
    pz = [device(at, xx, c, y) for at in zs]
    mine = group(c, xx, y)
    me = mine + z

    weights = []
    for k in range(CHUNKS):
        at = pl.ds(k * cols, cols)
        weights.append(
            [
                pltpu.make_async_copy(gate_hbm.at[:, :, at], wg.at[k], w_sem.at[0, k]),
                pltpu.make_async_copy(up_hbm.at[:, :, at], wu.at[k], w_sem.at[1, k]),
            ]
        )
    downs = [
        pltpu.make_async_copy(
            down_hbm.at[:, :, pl.ds(k * cols, cols)], wd.at[k], w_sem.at[2, k]
        )
        for k in range(CHUNKS)
    ]
    for pair in weights:
        for copy in pair:
            copy.start()
    for copy in downs:
        copy.start()

    barrier = pltpu.get_barrier_semaphore()
    for peer in (px, py, pc, pz[1], pz[2], pz[3]):
        pl.semaphore_signal(barrier, inc=1, device_id=peer, device_id_type=MESH)

    attend_in_vmem(
        q_ref, k_ref, v_ref, nk_ref, nv_ref, len_ref, heads, fresh_k, fresh_v, att
    )
    hid[...] = jnp.zeros_like(hid)
    for h in range(width // HD):
        hid[0 : steps * seqs, h * HD : (h + 1) * HD] = att[:, h, :]
    for step in range(steps):
        at = slice(step * seqs, (step + 1) * seqs)
        hid[at, :] = hid[at, :] + res_ref[step].astype(F32)
    hidden = hid[...]
    mean_square = jnp.mean(hidden * hidden, axis=-1, keepdims=True)
    normed = (hidden * lax.rsqrt(mean_square + 1e-06) * gain_ref[...].astype(F32).reshape(1, width)).astype(
        BF16
    )
    for k in range(CHUNKS):
        x[k, me] = normed[:, k * cols : (k + 1) * cols]
    own_gates[...] = jnp.zeros_like(own_gates)
    lane = lax.broadcasted_iota(jnp.int32, (seqs, HD), 1)
    for step in range(steps):
        chosen = ids_ref[step]
        score = score_ref[step].astype(F32)
        score = score / jnp.sum(score, axis=-1, keepdims=True)
        spread = jnp.zeros((seqs, HD), F32)
        for place in range(chosen.shape[1]):
            spread = spread + jnp.where(
                lane == chosen[:, place : place + 1], score[:, place : place + 1], 0.0
            )
        own_gates[step * seqs : (step + 1) * seqs, :] = spread
    gates[me] = own_gates[...]

    started = []

    def send(src, dst, sems, i, j, peer):
        copy = pltpu.make_async_remote_copy(
            src_ref=src, dst_ref=dst, send_sem=sems[0].at[i, j], recv_sem=sems[1].at[i, j],
            device_id=peer, device_id_type=MESH,
        )
        copy.start()
        started.append(copy)

    def arrive(ref, sems, i, j, peer):
        pltpu.make_async_remote_copy(
            src_ref=ref, dst_ref=ref, send_sem=sems[0].at[i, j], recv_sem=sems[1].at[i, j],
            device_id=peer, device_id_type=MESH,
        ).wait_recv()

    ag, rs = (ag_send, ag_recv), (rs_send, rs_recv)
    pl.semaphore_wait(barrier, 6)

    parts = [x.at[k] for k in range(CHUNKS)] + [gates]
    own, side_x = pl.ds(mine, 4), pl.ds(group(c, 1 - xx, y), 4)
    side_y, corner = pl.ds(group(c, xx, 1 - y), 4), pl.ds(group(c, 1 - xx, 1 - y), 4)
    others = [
        pl.ds(group(1 - c, xx, y), 4), pl.ds(group(1 - c, 1 - xx, y), 4),
        pl.ds(group(1 - c, xx, 1 - y), 4), pl.ds(group(1 - c, 1 - xx, 1 - y), 4),
    ]

    def gather_z(i):
        for dz in (1, 2, 3):
            send(parts[i].at[me], parts[i].at[me], ag, i, dz, pz[dz])

    def gather_a(i):
        for dz in (1, 2, 3):
            back = lax.rem(z + 4 - dz, 4)
            arrive(parts[i].at[mine + back], ag, i, dz, pz[4 - dz])
        send(parts[i].at[own], parts[i].at[own], ag, i, 4, px)
        send(parts[i].at[own], parts[i].at[own], ag, i, 5, py)
        send(parts[i].at[own], parts[i].at[own], ag, i, 6, pc)

    half = cols // 2
    halves = [pl.ds(h * half, half) for h in range(2)]

    def routed(i, rows):
        if i == CHUNKS:
            return [parts[i].at[rows]]
        return [parts[i].at[rows, :, at] for at in halves]

    def gather_b(i):
        arrive(parts[i].at[side_x], ag, i, 4, px)
        block = routed(i, side_x)[0]
        send(block, block, ag, i, 0, py)
        send(parts[i].at[side_x], parts[i].at[side_x], ag, i, 7, pc)
        arrive(parts[i].at[side_y], ag, i, 5, py)
        for block in routed(i, side_y)[1:]:
            send(block, block, ag, i, 10, px)
        send(parts[i].at[side_y], parts[i].at[side_y], ag, i, 8, pc)

    def gather_c(i):
        for block, at, peer in zip(routed(i, corner), (0, 10), (py, px)):
            arrive(block, ag, i, at, peer)
        send(parts[i].at[corner], parts[i].at[corner], ag, i, 9, pc)

    def gather_d(i):
        for n, at in enumerate(others):
            arrive(parts[i].at[at], ag, i, 6 + n, pc)

    def project(k):
        for copy in weights[k]:
            copy.wait()
        xk[...] = x[k].astype(F32).reshape(DEVICES * ROWS, cols).astype(BF16)

        @pl.loop(0, local)
        def _(e):
            tokens = xk[...]
            g = lax.dot_general(wg[k, e], tokens, NT, preferred_element_type=F32)
            u = lax.dot_general(wu[k, e], tokens, NT, preferred_element_type=F32)
            if k == 0:
                g_acc[e] = g
                u_acc[e] = u
            else:
                g_acc[e] += g
                u_acc[e] += u

    def project_last(k):
        for copy in weights[k]:
            copy.wait()
        xk[...] = x[k].astype(F32).reshape(DEVICES * ROWS, cols).astype(BF16)
        by_expert = gates[...].reshape(DEVICES * ROWS, HD).T
        row = lax.broadcasted_iota(jnp.int32, by_expert.shape, 0)
        tokens = xk[...]
        tile = 256
        for e in range(local):
            gate_row = jnp.sum(
                jnp.where(row == rep * local + e, by_expert, 0.0), axis=0, keepdims=True
            )
            g_all = lax.dot_general(wg[k, e], tokens, NT, preferred_element_type=F32)
            u_all = lax.dot_general(wu[k, e], tokens, NT, preferred_element_type=F32)
            for n in range(units // tile):
                at = slice(n * tile, (n + 1) * tile)
                g, u = g_acc[e, at, :] + g_all[at], u_acc[e, at, :] + u_all[at]
                value = g / (1.0 + jnp.exp(-g)) * u * gate_row
                first = e * units + n * tile
                act[:, first : first + tile] = value.T.astype(BF16)

    turns = [[0, CHUNKS]] + [[k] for k in range(1, CHUNKS)]
    for i in turns[0]:
        gather_z(i)
    for t in range(CHUNKS + 3):
        if t + 1 < CHUNKS:
            for i in turns[t + 1]:
                gather_z(i)
        for lag, stage in enumerate((gather_a, gather_b, gather_c, gather_d)):
            if 0 <= t - lag < CHUNKS:
                for i in turns[t - lag]:
                    stage(i)
        if 0 <= t - 3 < CHUNKS - 1:
            project(t - 3)
    project_last(CHUNKS - 1)

    def reduce_0(n):
        downs[n].wait()

        for h in range(2):
            at = slice(h * half, (h + 1) * half)
            part = jnp.dot(act[:, 0:units], wd[n, 0, :, at], preferred_element_type=F32)
            for e in range(1, local):
                part = part + jnp.dot(
                    act[:, e * units : (e + 1) * units], wd[n, e, :, at],
                    preferred_element_type=F32,
                )
            p[n, :, :, at] = part.reshape(DEVICES, ROWS, half).astype(BF16)
        send(p.at[n, pl.ds((1 - c) * 16, 16)], rc.at[n], rs, n, 0, pc)

    def add(target, values):
        total = target[...].astype(F32)
        for value in values:
            total = total + value[...].astype(F32)
        target[...] = total.astype(BF16)

    def reduce_1(n):
        arrive(rc.at[n], rs, n, 0, pc)
        add(p.at[n, pl.ds(c * 16, 16)], [rc.at[n]])
        for h, (peer, near) in enumerate(((px, side_x), (py, side_y))):
            at = halves[h]
            send(p.at[n, corner, :, at], r1.at[n, 0, :, :, at], rs, n, 1 + h, peer)
        for h, (peer, near) in enumerate(((px, side_x), (py, side_y))):
            at = halves[h]
            send(p.at[n, near, :, at], r1.at[n, 1, :, :, at], rs, n, 3 + h, peer)

    def reduce_2(n):
        for h, (peer, onward, far) in enumerate(((px, py, side_y), (py, px, side_x))):
            at = halves[h]
            arrive(r1.at[n, 0, :, :, at], rs, n, 1 + h, peer)
            add(p.at[n, far, :, at], [r1.at[n, 0, :, :, at]])
            send(p.at[n, far, :, at], r2.at[n, :, :, at], rs, n, 5 + h, onward)

    def reduce_3(n):
        for h, (peer, onward) in enumerate(((px, py), (py, px))):
            at = halves[h]
            arrive(r1.at[n, 1, :, :, at], rs, n, 3 + h, peer)
            arrive(r2.at[n, :, :, at], rs, n, 5 + h, onward)
        add(p.at[n, own], [r1.at[n, 1], r2.at[n]])
        for dz in (1, 2, 3):
            send(p.at[n, mine + zs[dz]], rz.at[n, dz], rs, n, 6 + dz, pz[dz])

    def reduce_4(n):
        at = slice(n * cols, (n + 1) * cols)
        total = p[n, me].astype(F32)
        for dz in (1, 2, 3):
            arrive(rz.at[n, dz], rs, n, 6 + dz, pz[4 - dz])
            total = total + rz[n, dz].astype(F32)
        total = total + hid[:, at]
        for step in range(steps):
            out_ref[step, :, at] = total[step * seqs : (step + 1) * seqs].astype(BF16)

    stages = (reduce_0, reduce_1, reduce_2, reduce_3, reduce_4)
    for t in range(CHUNKS + len(stages) - 1):
        for lag, stage in enumerate(stages):
            if 0 <= t - lag < CHUNKS:
                stage(t - lag)
    for copy in started:
        copy.wait_send()


def per_device_kernel(
    residual, queries, key_cache, value_cache, new_keys, new_values, cache_len, norm_gain,
    expert_ids, gate_scores, gate_weight, up_weight, down_weight,
):
    steps, seqs, width = residual.shape
    local, units, _ = gate_weight.shape
    cols = width // CHUNKS
    kv_heads = key_cache.shape[2] // HD
    heads = width // HD
    vmem = pl.BlockSpec(memory_space=pltpu.VMEM)
    hbm = pl.BlockSpec(memory_space=pl.ANY)
    smem = pl.BlockSpec(memory_space=pltpu.SMEM)
    rows = DEVICES * ROWS
    return pl.pallas_call(
        layer_kernel,
        out_shape=jax.ShapeDtypeStruct(residual.shape, BF16),
        in_specs=[vmem] * 6 + [smem] + [vmem] * 3 + [hbm] * 3,
        out_specs=vmem,
        scratch_shapes=[
            pltpu.VMEM((CHUNKS, local, units, cols), BF16),
            pltpu.VMEM((CHUNKS, local, units, cols), BF16),
            pltpu.VMEM((CHUNKS, local, units, cols), BF16),
            pltpu.VMEM((steps * seqs, heads, HD), F32),
            pltpu.VMEM((seqs * kv_heads, HD, HD), F32),
            pltpu.VMEM((seqs * kv_heads, HD, HD), F32),
            pltpu.VMEM((steps * seqs, heads, HD), F32),
            pltpu.VMEM((ROWS, width), F32),
            pltpu.VMEM((ROWS, HD), F32),
            pltpu.VMEM((CHUNKS, DEVICES, ROWS, cols), BF16),
            pltpu.VMEM((DEVICES, ROWS, HD), F32),
            pltpu.VMEM((rows, cols), BF16),
            pltpu.VMEM((local, units, rows), F32),
            pltpu.VMEM((local, units, rows), F32),
            pltpu.VMEM((rows, local * units), BF16),
            pltpu.VMEM((CHUNKS, DEVICES, ROWS, cols), BF16),
            pltpu.VMEM((CHUNKS, 16, ROWS, cols), BF16),
            pltpu.VMEM((CHUNKS, 2, 4, ROWS, cols), BF16),
            pltpu.VMEM((CHUNKS, 4, ROWS, cols), BF16),
            pltpu.VMEM((CHUNKS, 4, ROWS, cols), BF16),
            pltpu.SemaphoreType.DMA((3, CHUNKS)),
            pltpu.SemaphoreType.DMA((CHUNKS + 1, 11)),
            pltpu.SemaphoreType.DMA((CHUNKS + 1, 11)),
            pltpu.SemaphoreType.DMA((CHUNKS, 10)),
            pltpu.SemaphoreType.DMA((CHUNKS, 10)),
        ],
        compiler_params=pltpu.CompilerParams(
            collective_id=0, has_side_effects=True, vmem_limit_bytes=60 * 1024 * 1024
        ),
    )(
        residual, queries, key_cache, value_cache, new_keys, new_values, cache_len,
        norm_gain, expert_ids, gate_scores, gate_weight, up_weight,
        down_weight,
    )


def solution(mesh):
    in_specs = (
        P(None, ("rep", "exp"), None),
        P(None, ("rep", "exp"), None),
        P(("rep", "exp"), None, None),
        P(("rep", "exp"), None, None),
        P(None, ("rep", "exp"), None),
        P(None, ("rep", "exp"), None),
        P(("rep", "exp")),
        P(),
        P(None, ("rep", "exp"), None),
        P(None, ("rep", "exp"), None),
        P("rep", "exp", None),
        P("rep", "exp", None),
        P("rep", "exp", None),
    )
    out_specs = P(None, ("rep", "exp"), None)
    fits = mesh.shape["rep"] == 16 and mesh.shape["exp"] == 2
    per_device = per_device_kernel if fits else per_device_plain
    return jax.shard_map(
        per_device, mesh=mesh, in_specs=in_specs, out_specs=out_specs, check_vma=False
    )
```

```python
import math

import jax
import jax.numpy as jnp
from jax import lax
from jax.experimental import pallas as pl
from jax.experimental.pallas import tpu as pltpu
from jax.sharding import PartitionSpec as P

HD = 128


def attend_rows(queries, key_cache, value_cache, new_keys, new_values, cache_len):
    steps, rows, width = queries.shape
    cache = key_cache.shape[1]
    kv_heads = key_cache.shape[2] // HD
    group = width // HD // kv_heads
    scaling = 1.0 / math.sqrt(HD)
    heads = queries.reshape(steps, rows, kv_heads, group, HD).transpose(1, 2, 0, 3, 4)
    heads = heads.reshape(rows, kv_heads, steps * group, HD)
    keys = key_cache.reshape(rows, cache, kv_heads, HD)
    values = value_cache.reshape(rows, cache, kv_heads, HD)
    fresh_keys = new_keys.reshape(steps, rows, kv_heads, HD)
    fresh_values = new_values.reshape(steps, rows, kv_heads, HD)
    old = jnp.einsum("sjgd,stjd->sjgt", heads, keys, preferred_element_type=jnp.float32) * scaling
    new = (
        jnp.einsum("sjgd,tsjd->sjgt", heads, fresh_keys, preferred_element_type=jnp.float32)
        * scaling
    )
    position = lax.broadcasted_iota(jnp.int32, (1, 1, 1, cache), 3)
    old = jnp.where(position < cache_len[:, None, None, None], old, -1e30)
    step_of = lax.broadcasted_iota(jnp.int32, (1, 1, steps * group, steps), 2) // group
    fresh = lax.broadcasted_iota(jnp.int32, (1, 1, steps * group, steps), 3)
    new = jnp.where(fresh <= step_of, new, -1e30)
    top = jnp.maximum(
        jnp.max(old, axis=-1, keepdims=True), jnp.max(new, axis=-1, keepdims=True)
    )
    old, new = jnp.exp(old - top), jnp.exp(new - top)
    total = jnp.sum(old, axis=-1, keepdims=True) + jnp.sum(new, axis=-1, keepdims=True)
    old, new = (old / total).astype(jnp.bfloat16), (new / total).astype(jnp.bfloat16)
    out = jnp.einsum("sjgt,stjd->sjgd", old, values, preferred_element_type=jnp.float32)
    out = out + jnp.einsum(
        "sjgt,tsjd->sjgd", new, fresh_values, preferred_element_type=jnp.float32
    )
    out = out.reshape(rows, kv_heads, steps, group, HD).transpose(2, 0, 1, 3, 4)
    return out.reshape(steps, rows, width)


def norm_rows(hidden, norm_gain):
    mean_square = jnp.mean(hidden * hidden, axis=-1, keepdims=True)
    return (hidden * lax.rsqrt(mean_square + 1e-06) * norm_gain.astype(jnp.float32)).astype(
        jnp.bfloat16
    )


def per_device_plain(
    residual, queries, key_cache, value_cache, new_keys, new_values, cache_len, norm_gain,
    expert_ids, gate_scores, gate_weight, up_weight, down_weight,
):
    axes = ("rep", "exp")
    steps, rows, width = residual.shape
    local = gate_weight.shape[0]
    attention = attend_rows(queries, key_cache, value_cache, new_keys, new_values, cache_len)
    hidden = residual.astype(jnp.float32) + attention
    normed = norm_rows(hidden, norm_gain)
    scores = gate_scores.astype(jnp.float32)
    gates = scores / jnp.sum(scores, axis=-1, keepdims=True)
    tokens = lax.all_gather(normed.reshape(steps * rows, width), axes, axis=0, tiled=True)
    all_ids = lax.all_gather(expert_ids.reshape(steps * rows, -1), axes, axis=0, tiled=True)
    all_gates = lax.all_gather(gates.reshape(steps * rows, -1), axes, axis=0, tiled=True)
    mine = lax.axis_index("rep") * local + lax.broadcasted_iota(jnp.int32, (1, local, 1), 1)
    weight = jnp.sum(jnp.where(all_ids[:, None, :] == mine, all_gates[:, None, :], 0.0), axis=2)
    contract = (((1,), (1,)), ((), ()))
    units = gate_weight.shape[1]
    gate = lax.dot_general(
        tokens, gate_weight.reshape(local * units, width), contract,
        preferred_element_type=jnp.float32,
    )
    up = lax.dot_general(
        tokens, up_weight.reshape(local * units, width), contract,
        preferred_element_type=jnp.float32,
    )
    activation = (jax.nn.silu(gate) * up).reshape(-1, local, units) * weight[:, :, None]
    activation = activation.astype(jnp.bfloat16).reshape(-1, local * units)
    partial = jnp.dot(
        activation, down_weight.reshape(local * units, width), preferred_element_type=jnp.float32
    ).astype(jnp.bfloat16)
    mixed = lax.psum_scatter(partial, axes, scatter_dimension=0, tiled=True)
    mixed = mixed.reshape(steps, rows, width).astype(jnp.float32)
    return (hidden + mixed).astype(jnp.bfloat16)


CHUNKS = 4
ROWS = 8
DEVICES = 32
MESH = pl.DeviceIdType.MESH
F32 = jnp.float32
BF16 = jnp.bfloat16
NT = (((1,), (1,)), ((), ()))


def attend_in_vmem(
    q_ref, k_ref, v_ref, nk_ref, nv_ref, len_ref, heads, fresh_k, fresh_v, att, caches
):
    steps, seqs, width = q_ref.shape
    cache = k_ref.shape[1]
    kv_heads = k_ref.shape[2] // HD
    head_count = width // HD
    group = head_count // kv_heads
    scaling = 1.0 / math.sqrt(HD)
    for step in range(steps):
        rows = q_ref[step].astype(F32)
        for h in range(head_count):
            heads[step * seqs : (step + 1) * seqs, h, :] = rows[:, h * HD : (h + 1) * HD]
    fresh_k[...] = jnp.zeros_like(fresh_k)
    fresh_v[...] = jnp.zeros_like(fresh_v)
    for step in range(steps):
        key_rows = nk_ref[step].astype(F32)
        value_rows = nv_ref[step].astype(F32)
        for seq in range(seqs):
            for j in range(kv_heads):
                cols = slice(j * HD, (j + 1) * HD)
                at = seq * kv_heads + j
                fresh_k[at, step : step + 1, :] = key_rows[seq : seq + 1, cols]
                fresh_v[at, step : step + 1, :] = value_rows[seq : seq + 1, cols]
    for copy in caches:
        copy.wait()
    total = steps * group
    position = lax.broadcasted_iota(jnp.int32, (total, cache), 1)
    fresh_at = lax.broadcasted_iota(jnp.int32, (total, HD), 1)
    step_of = lax.broadcasted_iota(jnp.int32, (total, HD), 0) // group
    for seq in range(seqs):
        valid = position < len_ref[seq]
        for j in range(kv_heads):
            at = seq * kv_heads + j
            cols = slice(j * HD, (j + 1) * HD)
            query = jnp.concatenate(
                [
                    heads[step * seqs + seq, j * group : (j + 1) * group, :]
                    for step in range(steps)
                ],
                axis=0,
            ).astype(BF16)
            old = lax.dot_general(query, k_ref[seq, :, cols], NT, preferred_element_type=F32)
            new = lax.dot_general(
                query, fresh_k[at].astype(BF16), NT, preferred_element_type=F32
            )
            old = jnp.where(valid, old * scaling, -1e30)
            new = jnp.where(fresh_at <= step_of, new * scaling, -1e30)
            top = jnp.maximum(
                jnp.max(old, axis=-1, keepdims=True), jnp.max(new, axis=-1, keepdims=True)
            )
            old, new = jnp.exp(old - top), jnp.exp(new - top)
            share = 1.0 / (
                jnp.sum(old, axis=-1, keepdims=True) + jnp.sum(new, axis=-1, keepdims=True)
            )
            old, new = (old * share).astype(BF16), (new * share).astype(BF16)
            out = jnp.dot(old, v_ref[seq, :, cols], preferred_element_type=F32)
            out = out + jnp.dot(new, fresh_v[at].astype(BF16), preferred_element_type=F32)
            for step in range(steps):
                att[step * seqs + seq, j * group : (j + 1) * group, :] = out[
                    step * group : (step + 1) * group
                ]


def layer_kernel(
    res_ref, q_ref, k_hbm, v_hbm, nk_ref, nv_ref, len_ref, gain_ref, ids_ref, score_ref,
    gate_hbm, up_hbm, down_hbm,
    out_ref,
    k_ref, v_ref, wg, wu, wd, heads, fresh_k, fresh_v, att, hid, own_gates, x, gates, xk, g_acc, u_acc, act,
    p, rc, r1, r2, rz, w_sem, ag_send, ag_recv, rs_send, rs_recv,
):
    steps, seqs, width = res_ref.shape
    local, units = gate_hbm.shape[0], gate_hbm.shape[1]
    cols = width // CHUNKS
    rep, y = lax.axis_index("rep"), lax.axis_index("exp")
    c = lax.rem(rep, 2)
    xx = lax.rem(lax.div(rep, 2), 2)
    z = lax.div(rep, 4)

    def device(z_at, x_at, c_at, y_at):
        return ((z_at * 2 + x_at) * 2 + c_at, y_at)

    def group(c_at, x_at, y_at):
        return ((c_at * 2 + x_at) * 2 + y_at) * 4

    px, py, pc = device(z, 1 - xx, c, y), device(z, xx, c, 1 - y), device(z, xx, 1 - c, y)
    zs = [lax.rem(z + dz, 4) for dz in range(4)]
    pz = [device(at, xx, c, y) for at in zs]
    mine = group(c, xx, y)
    me = mine + z

    caches = [
        pltpu.make_async_copy(k_hbm, k_ref, w_sem.at[3, 0]),
        pltpu.make_async_copy(v_hbm, v_ref, w_sem.at[3, 1]),
    ]
    for copy in caches:
        copy.start()
    weights = []
    for k in range(CHUNKS):
        at = pl.ds(k * cols, cols)
        weights.append(
            [
                pltpu.make_async_copy(gate_hbm.at[:, :, at], wg.at[k], w_sem.at[0, k]),
                pltpu.make_async_copy(up_hbm.at[:, :, at], wu.at[k], w_sem.at[1, k]),
            ]
        )
    downs = [
        pltpu.make_async_copy(
            down_hbm.at[:, :, pl.ds(k * cols, cols)], wd.at[k], w_sem.at[2, k]
        )
        for k in range(CHUNKS)
    ]
    for pair in weights:
        for copy in pair:
            copy.start()
    for copy in downs:
        copy.start()

    barrier = pltpu.get_barrier_semaphore()
    for peer in (px, py, pc, pz[1], pz[2], pz[3]):
        pl.semaphore_signal(barrier, inc=1, device_id=peer, device_id_type=MESH)

    attend_in_vmem(
        q_ref, k_ref, v_ref, nk_ref, nv_ref, len_ref, heads, fresh_k, fresh_v, att, caches
    )
    hid[...] = jnp.zeros_like(hid)
    for h in range(width // HD):
        hid[0 : steps * seqs, h * HD : (h + 1) * HD] = att[:, h, :]
    for step in range(steps):
        at = slice(step * seqs, (step + 1) * seqs)
        hid[at, :] = hid[at, :] + res_ref[step].astype(F32)
    hidden = hid[...]
    mean_square = jnp.mean(hidden * hidden, axis=-1, keepdims=True)
    normed = (hidden * lax.rsqrt(mean_square + 1e-06) * gain_ref[...].astype(F32).reshape(1, width)).astype(
        BF16
    )
    for k in range(CHUNKS):
        x[k, me] = normed[:, k * cols : (k + 1) * cols]
    own_gates[...] = jnp.zeros_like(own_gates)
    lane = lax.broadcasted_iota(jnp.int32, (seqs, HD), 1)
    for step in range(steps):
        chosen = ids_ref[step]
        score = score_ref[step].astype(F32)
        score = score / jnp.sum(score, axis=-1, keepdims=True)
        spread = jnp.zeros((seqs, HD), F32)
        for place in range(chosen.shape[1]):
            spread = spread + jnp.where(
                lane == chosen[:, place : place + 1], score[:, place : place + 1], 0.0
            )
        own_gates[step * seqs : (step + 1) * seqs, :] = spread
    gates[me] = own_gates[...]

    started = []

    def send(src, dst, sems, i, j, peer):
        copy = pltpu.make_async_remote_copy(
            src_ref=src, dst_ref=dst, send_sem=sems[0].at[i, j], recv_sem=sems[1].at[i, j],
            device_id=peer, device_id_type=MESH,
        )
        copy.start()
        started.append(copy)

    def arrive(ref, sems, i, j, peer):
        pltpu.make_async_remote_copy(
            src_ref=ref, dst_ref=ref, send_sem=sems[0].at[i, j], recv_sem=sems[1].at[i, j],
            device_id=peer, device_id_type=MESH,
        ).wait_recv()

    ag, rs = (ag_send, ag_recv), (rs_send, rs_recv)
    pl.semaphore_wait(barrier, 6)

    parts = [x.at[k] for k in range(CHUNKS)] + [gates]
    own, side_x = pl.ds(mine, 4), pl.ds(group(c, 1 - xx, y), 4)
    side_y, corner = pl.ds(group(c, xx, 1 - y), 4), pl.ds(group(c, 1 - xx, 1 - y), 4)
    others = [
        pl.ds(group(1 - c, xx, y), 4), pl.ds(group(1 - c, 1 - xx, y), 4),
        pl.ds(group(1 - c, xx, 1 - y), 4), pl.ds(group(1 - c, 1 - xx, 1 - y), 4),
    ]

    def gather_z(i):
        for dz in (1, 2, 3):
            send(parts[i].at[me], parts[i].at[me], ag, i, dz, pz[dz])

    def gather_a(i):
        for dz in (1, 2, 3):
            back = lax.rem(z + 4 - dz, 4)
            arrive(parts[i].at[mine + back], ag, i, dz, pz[4 - dz])
        send(parts[i].at[own], parts[i].at[own], ag, i, 4, px)
        send(parts[i].at[own], parts[i].at[own], ag, i, 5, py)
        send(parts[i].at[own], parts[i].at[own], ag, i, 6, pc)

    half = cols // 2
    halves = [pl.ds(h * half, half) for h in range(2)]

    def routed(i, rows):
        if i == CHUNKS:
            return [parts[i].at[rows]]
        return [parts[i].at[rows, :, at] for at in halves]

    def gather_b(i):
        arrive(parts[i].at[side_x], ag, i, 4, px)
        block = routed(i, side_x)[0]
        send(block, block, ag, i, 0, py)
        send(parts[i].at[side_x], parts[i].at[side_x], ag, i, 7, pc)
        arrive(parts[i].at[side_y], ag, i, 5, py)
        for block in routed(i, side_y)[1:]:
            send(block, block, ag, i, 10, px)
        send(parts[i].at[side_y], parts[i].at[side_y], ag, i, 8, pc)

    def gather_c(i):
        for block, at, peer in zip(routed(i, corner), (0, 10), (py, px)):
            arrive(block, ag, i, at, peer)
        send(parts[i].at[corner], parts[i].at[corner], ag, i, 9, pc)

    def gather_d(i):
        for n, at in enumerate(others):
            arrive(parts[i].at[at], ag, i, 6 + n, pc)

    def project(k):
        for copy in weights[k]:
            copy.wait()
        xk[...] = x[k].astype(F32).reshape(DEVICES * ROWS, cols).astype(BF16)

        @pl.loop(0, local)
        def _(e):
            tokens = xk[...]
            g = lax.dot_general(wg[k, e], tokens, NT, preferred_element_type=F32)
            u = lax.dot_general(wu[k, e], tokens, NT, preferred_element_type=F32)
            if k == 0:
                g_acc[e] = g
                u_acc[e] = u
            else:
                g_acc[e] += g
                u_acc[e] += u

    def project_last(k):
        for copy in weights[k]:
            copy.wait()
        xk[...] = x[k].astype(F32).reshape(DEVICES * ROWS, cols).astype(BF16)
        by_expert = gates[...].reshape(DEVICES * ROWS, HD).T
        row = lax.broadcasted_iota(jnp.int32, by_expert.shape, 0)
        tokens = xk[...]
        tile = 256
        for e in range(local):
            gate_row = jnp.sum(
                jnp.where(row == rep * local + e, by_expert, 0.0), axis=0, keepdims=True
            )
            g_all = lax.dot_general(wg[k, e], tokens, NT, preferred_element_type=F32)
            u_all = lax.dot_general(wu[k, e], tokens, NT, preferred_element_type=F32)
            for n in range(units // tile):
                at = slice(n * tile, (n + 1) * tile)
                g, u = g_acc[e, at, :] + g_all[at], u_acc[e, at, :] + u_all[at]
                value = g / (1.0 + jnp.exp(-g)) * u * gate_row
                first = e * units + n * tile
                act[:, first : first + tile] = value.T.astype(BF16)

    turns = [[0, CHUNKS]] + [[k] for k in range(1, CHUNKS)]
    for i in turns[0]:
        gather_z(i)
    for t in range(CHUNKS + 3):
        if t + 1 < CHUNKS:
            for i in turns[t + 1]:
                gather_z(i)
        for lag, stage in enumerate((gather_a, gather_b, gather_c, gather_d)):
            if 0 <= t - lag < CHUNKS:
                for i in turns[t - lag]:
                    stage(i)
        if 0 <= t - 3 < CHUNKS - 1:
            project(t - 3)
    project_last(CHUNKS - 1)

    def reduce_0(n):
        downs[n].wait()

        for h in range(2):
            at = slice(h * half, (h + 1) * half)
            part = jnp.dot(act[:, 0:units], wd[n, 0, :, at], preferred_element_type=F32)
            for e in range(1, local):
                part = part + jnp.dot(
                    act[:, e * units : (e + 1) * units], wd[n, e, :, at],
                    preferred_element_type=F32,
                )
            p[n, :, :, at] = part.reshape(DEVICES, ROWS, half).astype(BF16)
        send(p.at[n, pl.ds((1 - c) * 16, 16)], rc.at[n], rs, n, 0, pc)

    def add(target, values):
        total = target[...].astype(F32)
        for value in values:
            total = total + value[...].astype(F32)
        target[...] = total.astype(BF16)

    def reduce_1(n):
        arrive(rc.at[n], rs, n, 0, pc)
        add(p.at[n, pl.ds(c * 16, 16)], [rc.at[n]])
        for h, (peer, near) in enumerate(((px, side_x), (py, side_y))):
            at = halves[h]
            send(p.at[n, corner, :, at], r1.at[n, 0, :, :, at], rs, n, 1 + h, peer)
        for h, (peer, near) in enumerate(((px, side_x), (py, side_y))):
            at = halves[h]
            send(p.at[n, near, :, at], r1.at[n, 1, :, :, at], rs, n, 3 + h, peer)

    def reduce_2(n):
        for h, (peer, onward, far) in enumerate(((px, py, side_y), (py, px, side_x))):
            at = halves[h]
            arrive(r1.at[n, 0, :, :, at], rs, n, 1 + h, peer)
            add(p.at[n, far, :, at], [r1.at[n, 0, :, :, at]])
            send(p.at[n, far, :, at], r2.at[n, :, :, at], rs, n, 5 + h, onward)

    def reduce_3(n):
        for h, (peer, onward) in enumerate(((px, py), (py, px))):
            at = halves[h]
            arrive(r1.at[n, 1, :, :, at], rs, n, 3 + h, peer)
            arrive(r2.at[n, :, :, at], rs, n, 5 + h, onward)
        add(p.at[n, own], [r1.at[n, 1], r2.at[n]])
        for dz in (1, 2, 3):
            send(p.at[n, mine + zs[dz]], rz.at[n, dz], rs, n, 6 + dz, pz[dz])

    def reduce_4(n):
        at = slice(n * cols, (n + 1) * cols)
        total = p[n, me].astype(F32)
        for dz in (1, 2, 3):
            arrive(rz.at[n, dz], rs, n, 6 + dz, pz[4 - dz])
            total = total + rz[n, dz].astype(F32)
        total = total + hid[:, at]
        for step in range(steps):
            out_ref[step, :, at] = total[step * seqs : (step + 1) * seqs]

    stages = (reduce_0, reduce_1, reduce_2, reduce_3, reduce_4)
    for t in range(CHUNKS + len(stages) - 1):
        for lag, stage in enumerate(stages):
            if 0 <= t - lag < CHUNKS:
                stage(t - lag)
    for copy in started:
        copy.wait_send()


def per_device_kernel(
    residual, queries, key_cache, value_cache, new_keys, new_values, cache_len, norm_gain,
    expert_ids, gate_scores, gate_weight, up_weight, down_weight,
):
    steps, seqs, width = residual.shape
    local, units, _ = gate_weight.shape
    cols = width // CHUNKS
    kv_heads = key_cache.shape[2] // HD
    heads = width // HD
    vmem = pl.BlockSpec(memory_space=pltpu.VMEM)
    hbm = pl.BlockSpec(memory_space=pl.ANY)
    smem = pl.BlockSpec(memory_space=pltpu.SMEM)
    rows = DEVICES * ROWS
    return pl.pallas_call(
        layer_kernel,
        out_shape=jax.ShapeDtypeStruct(residual.shape, F32),
        in_specs=[vmem] * 2 + [hbm] * 2 + [vmem] * 2 + [smem] + [vmem] * 3 + [hbm] * 3,
        out_specs=vmem,
        scratch_shapes=[
            pltpu.VMEM(key_cache.shape, BF16),
            pltpu.VMEM(value_cache.shape, BF16),
            pltpu.VMEM((CHUNKS, local, units, cols), BF16),
            pltpu.VMEM((CHUNKS, local, units, cols), BF16),
            pltpu.VMEM((CHUNKS, local, units, cols), BF16),
            pltpu.VMEM((steps * seqs, heads, HD), F32),
            pltpu.VMEM((seqs * kv_heads, HD, HD), F32),
            pltpu.VMEM((seqs * kv_heads, HD, HD), F32),
            pltpu.VMEM((steps * seqs, heads, HD), F32),
            pltpu.VMEM((ROWS, width), F32),
            pltpu.VMEM((ROWS, HD), F32),
            pltpu.VMEM((CHUNKS, DEVICES, ROWS, cols), BF16),
            pltpu.VMEM((DEVICES, ROWS, HD), F32),
            pltpu.VMEM((rows, cols), BF16),
            pltpu.VMEM((local, units, rows), F32),
            pltpu.VMEM((local, units, rows), F32),
            pltpu.VMEM((rows, local * units), BF16),
            pltpu.VMEM((CHUNKS, DEVICES, ROWS, cols), BF16),
            pltpu.VMEM((CHUNKS, 16, ROWS, cols), BF16),
            pltpu.VMEM((CHUNKS, 2, 4, ROWS, cols), BF16),
            pltpu.VMEM((CHUNKS, 4, ROWS, cols), BF16),
            pltpu.VMEM((CHUNKS, 4, ROWS, cols), BF16),
            pltpu.SemaphoreType.DMA((4, CHUNKS)),
            pltpu.SemaphoreType.DMA((CHUNKS + 1, 11)),
            pltpu.SemaphoreType.DMA((CHUNKS + 1, 11)),
            pltpu.SemaphoreType.DMA((CHUNKS, 10)),
            pltpu.SemaphoreType.DMA((CHUNKS, 10)),
        ],
        compiler_params=pltpu.CompilerParams(
            collective_id=0, has_side_effects=True, vmem_limit_bytes=60 * 1024 * 1024
        ),
    )(
        residual, queries, key_cache, value_cache, new_keys, new_values, cache_len,
        norm_gain, expert_ids, gate_scores, gate_weight, up_weight,
        down_weight,
    ).astype(BF16)


def solution(mesh):
    in_specs = (
        P(None, ("rep", "exp"), None),
        P(None, ("rep", "exp"), None),
        P(("rep", "exp"), None, None),
        P(("rep", "exp"), None, None),
        P(None, ("rep", "exp"), None),
        P(None, ("rep", "exp"), None),
        P(("rep", "exp")),
        P(),
        P(None, ("rep", "exp"), None),
        P(None, ("rep", "exp"), None),
        P("rep", "exp", None),
        P("rep", "exp", None),
        P("rep", "exp", None),
    )
    out_specs = P(None, ("rep", "exp"), None)
    fits = mesh.shape["rep"] == 16 and mesh.shape["exp"] == 2
    per_device = per_device_kernel if fits else per_device_plain
    return jax.shard_map(
        per_device, mesh=mesh, in_specs=in_specs, out_specs=out_specs, check_vma=False
    )
```
